256 devices in a mesh: row: 4 (over x_hi, core), col: 8 (over z), depth: 8 (over y, x_lo).
Axes of the slice: x: 4 (x_hi: 2, x_lo: 2; x = x_hi * 2 + x_lo), y: 4, z: 8, core: 2. Of those that a mesh axis runs over, the one named last changes fastest.
Arguments:
- block_values: bfloat16 [192, 16, 128, 128], P(('row', 'depth'), 'col'), may hold values from -1.1953125 to 1.1953125
- block_columns: int32 [192, 16], P(('row', 'depth'), 'col'), may hold values from -1 to 23, as said below
- pattern_columns: int32 [192, 24], P('row', 'col'), may hold values from 0 to 23, as said below
Outputs:
- next_values: bfloat16 [192, 24, 128, 128], P(('row', 'depth'), 'col')
The draws below stay inside these ranges and needn't reach their ends.
Inputs may be any that keep to these rules, and one draw needn't show every extreme that they name: `block_columns`: in each block row and panel the 2 slots first list distinct block columns of that panel, numbered from 0 within it, then hold -1; at least one slot is used; the listed columns are the first entries of pattern_columns in that block row and panel, in the same order. `pattern_columns`: in each block row and panel the 3 entries are distinct block columns of that panel, numbered from 0 within it.
All inputs are finite; a program needn't handle non-finite values.
Results may differ from the reference program's by a relative error of at most 0.012.
Values may be sent and summed in bfloat16 or wider, within the bound.
No kernel may reach another device: no remote copies, remote signals or barrier semaphores. Data moves between devices by JAX's collectives and lax.ppermute only.
A program may use at most 128 MiB of HBM per device.

```python
import jax
import jax.numpy as jnp
from jax import lax

NB = 192
BLK = 128
KA = 2
KC = 3
NPAN = 8
TP = 24
N_DEPTH = 8


def shuffle_panel(panel_key):
    return jax.random.permutation(panel_key, TP)


def pattern_tables(key):
    panel_keys = jax.random.split(key, NB * NPAN)
    orders = jax.vmap(shuffle_panel)(panel_keys).astype(jnp.int32).reshape(NB, NPAN, TP)
    pattern = orders[:, :, :KC]
    counts = jax.random.randint(jax.random.fold_in(key, 11), (NB, NPAN), 1, KA + 1)
    heavy = jax.random.randint(jax.random.fold_in(key, 12), (NB, 1), 0, 4) == 0
    forced = jax.random.randint(jax.random.fold_in(key, 13), (), 0, NB)
    heavy = heavy | (jnp.arange(NB) == forced)[:, None]
    counts = jnp.where(heavy, KA, counts)
    slot_range = jnp.arange(KA)
    listed = jnp.where(slot_range[None, None, :] < counts[:, :, None], orders[:, :, :KA], -1)
    return (listed.reshape(NB, NPAN * KA).astype(jnp.int32), pattern.reshape(NB, NPAN * KC).astype(jnp.int32))


def draw_block_columns(key, part):
    listed, pattern = pattern_tables(key)
    return listed


def draw_pattern_columns(key, part):
    listed, pattern = pattern_tables(key)
    return pattern


def level_of(stream_key, extent, shards, low, largest):
    loudness, own = 1.0, jax.random.fold_in(stream_key, 6)
    for axis_at, parts in shards:
        heights = jnp.exp(jax.random.uniform(jax.random.fold_in(own, axis_at), (parts,), jnp.float32, low / len(shards), largest / len(shards)))
        loudness = loudness * jnp.repeat(heights, extent[axis_at] // parts).reshape([-1 if axis == axis_at else 1 for axis in range(len(extent))])
    return loudness


def bell_draw(key, dims, scale, limit, shards=(), held_as=jnp.bfloat16):
    values = scale * jax.random.normal(key, dims, jnp.float32)
    if shards:
        values = values * level_of(key, dims, shards, -0.22, 0.18)
    return jnp.clip(values, -limit, limit).astype(held_as)


def setup_inputs(seed: int = 0) -> dict:
    key_of = jax.random.split(jax.random.key(seed), 4)
    return {
        "block_values": bell_draw(key_of[0], (NB, NPAN * KA, BLK, BLK), 0.2, 1.1953125, ((0, 32), (1, 8))),
        "block_columns": draw_block_columns(jax.random.fold_in(key_of[3], 71), 0),
        "pattern_columns": draw_pattern_columns(jax.random.fold_in(key_of[3], 71), 0),
    }


def product_rows(left_blocks, left_columns, right_blocks, right_columns, pattern, right_slots):
    out_slots = pattern.shape[1]
    left_slots = left_blocks.shape[1]
    right_count = right_columns.shape[1]
    slot_panel = jnp.arange(left_slots, dtype=jnp.int32) // KA
    right_panel = jnp.arange(right_count, dtype=jnp.int32) // right_slots
    out_panel = jnp.arange(out_slots, dtype=jnp.int32) // KC
    same_panel = right_panel[None, :] == out_panel[:, None]
    places = jnp.arange(right_count, dtype=jnp.int32)

    def one_row(row_index):
        blocks = left_blocks[row_index].astype(jnp.float32)
        columns = left_columns[row_index]
        wanted = pattern[row_index]
        source_rows = (slot_panel * TP + jnp.maximum(columns, 0)).astype(jnp.int32)
        chosen_blocks = right_blocks[source_rows].astype(jnp.float32)
        chosen_columns = right_columns[source_rows]
        products = jnp.einsum("sxy,styz->stxz", blocks, chosen_blocks)
        matches = (chosen_columns[:, None, :] == wanted[None, :, None]) & same_panel[None, :, :] & (columns >= 0)[:, None, None]
        position = jnp.sum(jnp.where(matches, places[None, None, :], 0), axis=2).astype(jnp.int32)
        found = jnp.any(matches, axis=2)
        index_table = jnp.broadcast_to(position[:, :, None, None], (left_slots, out_slots) + products.shape[2:])
        taken = jnp.take_along_axis(products, index_table, axis=1)
        terms = jnp.where(found[:, :, None, None], taken, 0.0)
        layered = jnp.sum(terms.reshape((N_DEPTH, left_slots // N_DEPTH, out_slots) + products.shape[2:]), axis=1)
        rounded = lax.optimization_barrier(layered.astype(jnp.bfloat16)).astype(jnp.float32)
        return jnp.sum(rounded, axis=0)

    return lax.map(one_row, jnp.arange(left_blocks.shape[0], dtype=jnp.int32))


def reference(block_values, block_columns, pattern_columns):
    square = product_rows(block_values, block_columns, block_values, block_columns, pattern_columns, KA).astype(jnp.bfloat16)
    cube_sum = product_rows(block_values, block_columns, square, pattern_columns, pattern_columns, KC)
    slot_panel = jnp.arange(block_columns.shape[1], dtype=jnp.int32) // KA
    out_panel = jnp.arange(pattern_columns.shape[1], dtype=jnp.int32) // KC
    matched = (block_columns[:, None, :] == pattern_columns[:, :, None]) & (slot_panel[None, None, :] == out_panel[None, :, None]) & (block_columns >= 0)[:, None, :]
    mapped = jnp.einsum("ius,isxy->iuxy", matched.astype(jnp.float32), block_values.astype(jnp.float32))
    return (1.5 * mapped - 0.5 * cube_sum).astype(jnp.bfloat16)
```

```python
import functools

import jax
import jax.numpy as jnp
from jax import lax
from jax.experimental import pallas as pl
from jax.experimental.pallas import tpu as pltpu
from jax.sharding import PartitionSpec as P

BLK = 128
KA = 2
KC = 3
TP = 24
ROWS = 6
PAY = ROWS * KA * BLK + 16
SROWS = ROWS * KC * BLK
HELD = 96
SLOTS = 48
ALL = ("row", "col", "depth")


def chip_of(device):
    row, col, depth = device // 64, device // 8 % 8, device % 8
    return row // 2 * 2 + depth % 2, depth // 2, col, row % 2


def device_of(x, y, z, core):
    return (x // 2 * 2 + core) * 64 + z * 8 + y * 2 + x % 2


def moves(rule):
    pairs = []
    for device in range(256):
        x, y, z, core = rule(*chip_of(device))
        pairs.append((device, device_of(x % 4, y % 4, z, core)))
    return pairs


def first_ring(step):
    return moves(lambda x, y, z, core: (x + step * (1 - core), y + step * core, z, core))


def second_ring(step):
    return moves(lambda x, y, z, core: (x + step * core, y + step * (1 - core), z, core))


def swap(array):
    return lax.ppermute(array, ALL, moves(lambda x, y, z, core: (x, y, z, 1 - core)))


def plane_gather(piece):
    ring = [piece] + [lax.ppermute(piece, ALL, first_ring(step)) for step in (1, -1, 2)]
    near = jnp.concatenate(ring, axis=0)
    half = near.shape[0] // 2
    plus = lax.ppermute(near, ALL, second_ring(1))
    minus = lax.ppermute(near, ALL, second_ring(-1))
    far_a = lax.ppermute(plus[:half], ALL, second_ring(1))
    far_b = lax.ppermute(minus[half:], ALL, second_ring(-1))
    return near, plus, minus, far_a, far_b


def product_kernel(
    slots, piece_rows, core_ref, place_ref, have_ref, want_ref, right_ref, find_ref,
    own_ref, other_ref, near_ref, plus_ref, minus_ref, fara_ref, farb_ref,
    mine_out, theirs_out, total, left_buf, right_buf, todo, count, sems,
):
    core = core_ref[0]
    count[0] = 0

    def wait(n):
        slot = lax.rem(n, SLOTS)
        pltpu.make_async_copy(own_ref.at[pl.ds(0, BLK)], left_buf.at[slot], sems.at[0, slot]).wait()
        pltpu.make_async_copy(own_ref.at[pl.ds(0, BLK)], right_buf.at[slot], sems.at[1, slot]).wait()

    def start(n):
        slot = lax.rem(n, SLOTS)
        entry = todo[0, n]
        row, spot = entry // 8, lax.rem(entry, 8)
        panel, side = spot // 2, lax.rem(spot, 2)

        def left(ref, offset):
            offset = pl.multiple_of(offset, 16)
            pltpu.make_async_copy(ref.at[pl.ds(offset, BLK)], left_buf.at[slot], sems.at[0, slot]).start()

        @pl.when(row < ROWS)
        def _():
            whole = panel // 2 * 4 + 2 * core + lax.rem(panel, 2)
            left(own_ref, whole * PAY + (row * KA + side) * BLK)

        @pl.when(row >= ROWS)
        def _():
            left(other_ref, panel * PAY + ((row - ROWS) * KA + side) * BLK)

        place = todo[1, n]
        group, line = place // ROWS, lax.rem(place, ROWS)
        outer, inner = group // 4, lax.rem(group, 4)
        block = (line * slots + todo[2, n]) * BLK

        def right(ref, offset):
            offset = pl.multiple_of(offset, 16)
            pltpu.make_async_copy(ref.at[pl.ds(offset, BLK)], right_buf.at[slot], sems.at[1, slot]).start()

        for index, ref in enumerate((near_ref, plus_ref, minus_ref)):
            pl.when(outer == index)(functools.partial(right, ref, inner * piece_rows + block))
        pl.when((outer == 3) & (inner < 2))(functools.partial(right, fara_ref, inner * piece_rows + block))
        pl.when((outer == 3) & (inner >= 2))(functools.partial(right, farb_ref, (inner - 2) * piece_rows + block))

    def scan_row(row, carry):
        for spot in range(8):
            entry = row * 8 + spot
            place = place_ref[entry]

            @pl.when((have_ref[place] & want_ref[row]) != 0)
            def _():
                for slot in range(slots):
                    column = right_ref[place * slots + slot]
                    found = find_ref[row * TP + jnp.maximum(column, 0)]

                    @pl.when((column >= 0) & (found >= 0))
                    def _():
                        n = count[0]
                        todo[0, n] = entry
                        todo[1, n] = place
                        todo[2, n] = slot
                        todo[3, n] = row * KC + found
                        count[0] = n + 1
                        pl.when(n < SLOTS)(functools.partial(start, n))

        return carry

    lax.fori_loop(0, 2 * ROWS, scan_row, 0)
    total[...] = jnp.zeros_like(total)
    found = count[0]

    def multiply(n, carry):
        wait(n)
        slot = lax.rem(n, SLOTS)
        out = todo[3, n]
        total[out] += jnp.dot(left_buf[slot], right_buf[slot], preferred_element_type=jnp.float32)
        pl.when(n + SLOTS < found)(functools.partial(start, n + SLOTS))
        return carry

    lax.fori_loop(0, found, multiply, 0)
    for block in range(ROWS * KC):
        mine_out[pl.ds(block * BLK, BLK), :] = total[block]
        theirs_out[pl.ds(block * BLK, BLK), :] = total[ROWS * KC + block].astype(jnp.bfloat16)


def product(slots, piece_rows, tables, arrays):
    smem = pl.BlockSpec(memory_space=pltpu.SMEM)
    hbm = pl.BlockSpec(memory_space=pl.ANY)
    vmem = pl.BlockSpec(memory_space=pltpu.VMEM)
    return pl.pallas_call(
        functools.partial(product_kernel, slots, piece_rows),
        out_shape=(
            jax.ShapeDtypeStruct((SROWS, BLK), jnp.float32),
            jax.ShapeDtypeStruct((SROWS, BLK), jnp.bfloat16),
        ),
        in_specs=[smem] * len(tables) + [hbm] * len(arrays),
        out_specs=(vmem, vmem),
        scratch_shapes=[
            pltpu.VMEM((2 * ROWS * KC, BLK, BLK), jnp.float32),
            pltpu.VMEM((SLOTS, BLK, BLK), jnp.bfloat16),
            pltpu.VMEM((SLOTS, BLK, BLK), jnp.bfloat16),
            pltpu.SMEM((4, 2 * ROWS * 8 * KC), jnp.int32),
            pltpu.SMEM((1,), jnp.int32),
            pltpu.SemaphoreType.DMA((2, SLOTS)),
        ],
        compiler_params=pltpu.CompilerParams(vmem_limit_bytes=24 * 1024 * 1024),
    )(*tables, *arrays)


def bits(columns):
    return jnp.sum(jnp.where(columns >= 0, 1 << jnp.maximum(columns, 0), 0), axis=-1, dtype=jnp.int32)


def local(block_values, block_columns, pattern_columns):
    row, depth = lax.axis_index("row"), lax.axis_index("depth")
    core, x, y = row % 2, row // 2 * 2 + depth % 2, depth // 2
    own_pattern = lax.dynamic_slice_in_dim(pattern_columns, depth * ROWS, ROWS, 0)

    marks = jnp.concatenate([block_columns.reshape(1, -1), own_pattern.reshape(1, -1)], axis=1)
    marks = jnp.pad(marks.astype(jnp.bfloat16), ((0, 15), (0, BLK - marks.shape[1])))
    piece = jnp.concatenate([block_values.reshape(ROWS * KA * BLK, BLK), marks], axis=0)

    left = lax.all_gather(piece, "col", axis=0, tiled=True)
    right = plane_gather(piece)
    wanted = jnp.concatenate([own_pattern, swap(own_pattern)], axis=0)

    by_core = left.reshape(2, 2, 2, PAY, BLK)
    left_other = swap(lax.dynamic_index_in_dim(by_core, 1 - core, 1, keepdims=False).reshape(4 * PAY, BLK))

    def marks_of(array):
        return array.reshape(-1, PAY, BLK)[:, ROWS * KA * BLK, :].astype(jnp.int32)

    own_marks = lax.dynamic_index_in_dim(marks_of(left).reshape(2, 2, 2, BLK), core, 1, keepdims=False)
    left_marks = jnp.stack([own_marks.reshape(4, BLK), marks_of(left_other)])[:, :, : ROWS * KA]
    left_columns = left_marks.reshape(2, 4, ROWS, KA).transpose(0, 2, 1, 3).reshape(2 * ROWS, 4, KA)

    panel, column = jnp.arange(4)[:, None], jnp.arange(TP)[None, :]
    away_x = (x - (panel // 2 * 2 + column // ROWS % 2)) % 4
    away_y = (y - (panel % 2 * 2 + column // 12)) % 4
    order = lambda away: jnp.where(away == 2, 3, jnp.where(away == 3, 2, away))
    away_x, away_y = order(away_x), order(away_y)
    group = jnp.where(core == 0, away_y * 4 + away_x, away_x * 4 + away_y)
    held_at = (group * ROWS + column % ROWS).astype(jnp.int32)
    hit = left_columns[:, :, :, None] == jnp.arange(TP)
    place = jnp.sum(jnp.where(hit, held_at[None, :, None, :], 0), axis=-1)
    place = jnp.where(left_columns >= 0, place, HELD).reshape(-1).astype(jnp.int32)

    right_marks = jnp.concatenate([marks_of(part) for part in right], axis=0)
    x_columns = right_marks[:, : ROWS * KA].reshape(HELD, KA)
    s_columns = right_marks[:, ROWS * KA : ROWS * (KA + KC)].reshape(HELD, KC)
    find = sum(jnp.where(wanted[:, u : u + 1] == jnp.arange(TP), u + 1, 0) for u in range(KC)) - 1
    want = bits(wanted)
    core_table = core.reshape(1).astype(jnp.int32)

    def tables(columns):
        have = jnp.pad(bits(columns), (0, 1))
        return core_table, place, have, want, columns.reshape(-1), find.reshape(-1).astype(jnp.int32)

    mine, theirs = product(KA, PAY, tables(x_columns), (left, left_other) + right)
    square = (mine + swap(theirs).astype(jnp.float32)).astype(jnp.bfloat16)
    mine, theirs = product(KC, SROWS, tables(s_columns), (left, left_other) + plane_gather(square))
    cube = (mine + swap(theirs).astype(jnp.float32)).reshape(ROWS, KC, BLK, BLK)
    stored = jnp.where((block_columns >= 0)[:, :, None, None], block_values, 0).astype(jnp.float32)
    mapped = jnp.pad(stored, ((0, 0), (0, KC - KA), (0, 0), (0, 0)))
    return (1.5 * mapped - 0.5 * cube).astype(jnp.bfloat16)


def solution(mesh):
    placed = (P(("row", "depth"), "col", None, None), P(("row", "depth"), "col"), P("row", "col"))
    return jax.shard_map(
        local,
        mesh=mesh,
        in_specs=placed,
        out_specs=P(("row", "depth"), "col", None, None),
        check_vma=False,
    )
```

```python
import functools

import jax
import jax.numpy as jnp
from jax import lax
from jax.experimental import pallas as pl
from jax.experimental.pallas import tpu as pltpu
from jax.sharding import PartitionSpec as P

BLK = 128
KA = 2
KC = 3
TP = 24
ROWS = 6
OUTS = ROWS * KC
LEFT = ROWS * KA
ROOM = 24
SLOTS = 64
JOBS = 2 * ROWS * 8 * KC
ALL = ("row", "col", "depth")


def chip_of(device):
    row, col, depth = device // 64, device // 8 % 8, device % 8
    return row // 2 * 2 + depth % 2, depth // 2, col, row % 2


def device_of(x, y, z, core):
    return (x // 2 * 2 + core) * 64 + z * 8 + y * 2 + x % 2


def move(array, rule):
    pairs = []
    for device in range(256):
        x, y, z, core = rule(*chip_of(device))
        pairs.append((device, device_of(x % 4, y % 4, z % 8, core)))
    return lax.ppermute(array, ALL, pairs)


def first_ring(array, step):
    return move(array, lambda x, y, z, core: (x + step * (1 - core), y + step * core, z, core))


def second_ring(array, step):
    return move(array, lambda x, y, z, core: (x + step * core, y + step * (1 - core), z, core))


def swap(array):
    return move(array, lambda x, y, z, core: (x, y, z, 1 - core))


def ring_order(away):
    away = away & 3
    return jnp.where(away == 2, 3, jnp.where(away == 3, 2, away))


def first_pieces(piece):
    return tuple([piece] + [first_ring(piece, step) for step in (1, -1, 2)])


def far_pieces(plus, minus):
    half = plus.shape[0] // 2
    return second_ring(plus[:half], 1), second_ring(minus[half:], -1)


def doubled(array, count, rule):
    return jnp.concatenate([array, move(array, functools.partial(rule, count))], axis=0)


def along_z(n, x, y, z, core):
    return x, y, z - n, core


def along_x(n, x, y, z, core):
    return x - n, y, z, core


def along_y(n, x, y, z, core):
    return x, y - n, z, core


def block_copy(ref, block, target, sem):
    offset = pl.multiple_of(block * BLK, BLK)
    return pltpu.make_async_copy(ref.at[pl.ds(offset, BLK)], target, sem)


def plan_kernel(here_ref, own_ref, other_ref, plane_ref, x_jobs, s_jobs, takes, seen, group_code):
    core, x, y, z = here_ref[0], here_ref[1], here_ref[2], here_ref[3]
    first, second = jnp.where(core == 0, x, y), jnp.where(core == 0, y, x)

    for group in range(16):
        at_x, at_y = group // 8 * 2 + group % 2, group // 4 % 2 * 2 + group // 2 % 2
        far = jnp.where(core == 0, at_x, at_y)
        inner = ring_order(first - far)
        outer = ring_order(second - jnp.where(core == 0, at_y, at_x))
        group_code[0, group] = inner
        group_code[1, group] = outer
        group_code[2, group] = far
        group_code[3, group] = ((at_y - y) & 3) * 4 + ((at_x - x) & 3)

    def clear(n, carry):
        seen[n] = -1
        return carry

    lax.fori_loop(0, 16 * OUTS, clear, 0)
    x_jobs[0] = 0
    s_jobs[0] = 0
    for outer in range(4):
        takes[outer, ROOM] = 0

    def scan(marks_ref, half):
        def scan_row(row, carry):
            wanted = [marks_ref[0, LEFT + row * KC + u] for u in range(KC)]
            for panel in range(4):
                whole = panel // 2 * 4 + 2 * core + panel % 2
                line = (whole - z) & 7
                for side in range(KA):
                    column = marks_ref[line, row * KA + side]

                    @pl.when(column >= 0)
                    def _(panel=panel, whole=whole, side=side, column=column):
                        quarter = column // ROWS
                        place = column - quarter * ROWS
                        group = panel * 4 + quarter
                        table = group_code[3, group]
                        founds = []
                        for slot in range(KC):
                            have = plane_ref[table, LEFT + place * KC + slot]
                            found = jnp.where(have == wanted[0], 0, jnp.where(have == wanted[1], 1, 2))
                            founds.append(jnp.where((found < 2) | (have == wanted[2]), found, -1))

                        @pl.when((founds[0] >= 0) | (founds[1] >= 0) | (founds[2] >= 0))
                        def _():
                            inner, outer = group_code[0, group], group_code[1, group]
                            left = half * 8 * LEFT + whole * LEFT + row * KA + side
                            source = jnp.where(outer < 3, outer, 3 + (inner >> 1))
                            within = jnp.where(outer < 3, inner, inner & 1) * ROWS + place
                            for slot, found in enumerate(founds):
                                out = half * OUTS + row * KC + found

                                if slot < KA:

                                    @pl.when((found >= 0) & (plane_ref[table, place * KA + slot] >= 0))
                                    def _(slot=slot, out=out):
                                        count = x_jobs[0]
                                        x_jobs[0] = count + 1
                                        block = within * KA + slot
                                        x_jobs[1 + count] = (source << 21) | (block << 14) | (left << 6) | out

                                @pl.when(found >= 0)
                                def _(slot=slot, out=out):
                                    mark = group * OUTS + place * KC + slot

                                    @pl.when((outer > 0) & (seen[mark] < 0))
                                    def _():
                                        rank = takes[outer, ROOM]
                                        takes[outer, ROOM] = rank + 1
                                        seen[mark] = rank

                                        @pl.when(rank < ROOM)
                                        def _():
                                            takes[outer, rank] = (group_code[2, group] << 5) | (place * KC + slot)

                                    count = s_jobs[0]
                                    s_jobs[0] = count + 1
                                    s_jobs[1 + count] = (source << 21) | ((within * KC + slot) << 14) | (left << 6) | out
                                    s_jobs[1 + JOBS + count] = jnp.where(
                                        outer == 0, (inner << 5) | (place * KC + slot), ((3 + outer) << 5) | (seen[mark] & 31)
                                    )

            return carry

        lax.fori_loop(0, ROWS, scan_row, 0)

    scan(own_ref, 0)
    scan(other_ref, 1)
    most = jnp.maximum(takes[1, ROOM], jnp.maximum(takes[2, ROOM], takes[3, ROOM]))
    for outer in range(4):
        takes[outer, ROOM + 1] = most


SMEM = pl.BlockSpec(memory_space=pltpu.SMEM)
VMEM = pl.BlockSpec(memory_space=pltpu.VMEM)
ANY = pl.BlockSpec(memory_space=pl.ANY)


def plan(here, own, other, plane):
    return pl.pallas_call(
        plan_kernel,
        out_shape=(
            jax.ShapeDtypeStruct((1 + JOBS,), jnp.int32),
            jax.ShapeDtypeStruct((1 + 2 * JOBS,), jnp.int32),
            jax.ShapeDtypeStruct((4, BLK), jnp.int32),
        ),
        in_specs=[SMEM] * 4,
        out_specs=(SMEM,) * 3,
        scratch_shapes=[pltpu.SMEM((16 * OUTS,), jnp.int32), pltpu.SMEM((4, 16), jnp.int32)],
    )(here, own, other, plane)


def product_kernel(rights, packed, jobs_ref, own_ref, other_ref, *refs):
    right_refs, (mine_out, theirs_out, total, left_buf, right_buf, sems) = refs[:rights], refs[rights:]
    count = jobs_ref[0]

    def start(n):
        slot = lax.rem(n, SLOTS)
        job = jobs_ref[1 + n]
        left = (job >> 6) & 255
        if packed:
            code = jobs_ref[1 + JOBS + n]
            source, block = code >> 5, code & 31
        else:
            source, block = job >> 21, (job >> 14) & 127

        @pl.when(left < 8 * LEFT)
        def _():
            block_copy(own_ref, left, left_buf.at[slot], sems.at[0, slot]).start()

        @pl.when(left >= 8 * LEFT)
        def _():
            block_copy(other_ref, left - 8 * LEFT, left_buf.at[slot], sems.at[0, slot]).start()

        for index, ref in enumerate(right_refs):

            @pl.when(source == index)
            def _(ref=ref):
                block_copy(ref, block, right_buf.at[slot], sems.at[1, slot]).start()

    def wait(n):
        slot = lax.rem(n, SLOTS)
        block_copy(own_ref, 0, left_buf.at[slot], sems.at[0, slot]).wait()
        block_copy(own_ref, 0, right_buf.at[slot], sems.at[1, slot]).wait()

    def first(n, carry):
        start(n)
        return carry

    lax.fori_loop(0, jnp.minimum(count, SLOTS), first, 0)
    total[...] = jnp.zeros_like(total)

    def multiply(group, carry):
        at = [group * 4 + index for index in range(4)]
        for n in at:
            pl.when(n < count)(functools.partial(wait, n))
        outs = [jnp.where(n < count, jobs_ref[jnp.minimum(1 + n, JOBS)] & 63, 2 * OUTS) for n in at]
        slots = [lax.rem(n, SLOTS) for n in at]
        dots = [jnp.dot(left_buf[slot], right_buf[slot], preferred_element_type=jnp.float32) for slot in slots]
        for out, dot in zip(outs, dots):
            total[out] += dot
        for n in at:
            pl.when(n + SLOTS < count)(functools.partial(start, n + SLOTS))
        return carry

    lax.fori_loop(0, (count + 3) // 4, multiply, 0)
    for block in range(OUTS):
        mine_out[pl.ds(block * BLK, BLK), :] = total[block]
        theirs_out[pl.ds(block * BLK, BLK), :] = total[OUTS + block].astype(jnp.bfloat16)


def product(jobs, left, left_other, rights, packed):
    return pl.pallas_call(
        functools.partial(product_kernel, len(rights), packed),
        out_shape=(
            jax.ShapeDtypeStruct((OUTS * BLK, BLK), jnp.float32),
            jax.ShapeDtypeStruct((OUTS * BLK, BLK), jnp.bfloat16),
        ),
        in_specs=[SMEM] + [ANY] * (2 + len(rights)),
        out_specs=(VMEM, VMEM),
        scratch_shapes=[
            pltpu.VMEM((2 * OUTS + 1, BLK, BLK), jnp.float32),
            pltpu.VMEM((SLOTS, BLK, BLK), jnp.bfloat16),
            pltpu.VMEM((SLOTS, BLK, BLK), jnp.bfloat16),
            pltpu.SemaphoreType.DMA((2, SLOTS)),
        ],
        compiler_params=pltpu.CompilerParams(vmem_limit_bytes=24 * 1024 * 1024),
    )(jobs, left, left_other, *rights)


def pack_kernel(here_ref, *refs):
    lists, pieces, outs, sems = refs[:3], refs[3:7], refs[7:10], refs[10]
    first = jnp.where(here_ref[0] == 0, here_ref[1], here_ref[2])

    for target, out in enumerate(outs):
        asked = lists[target]

        def start(n, carry, target=target, out=out, asked=asked):
            code = asked[0, n]
            inner = ring_order(first - (code >> 5))
            offset = pl.multiple_of(n * BLK, BLK)
            for index, ref in enumerate(pieces):

                @pl.when(inner == index)
                def _(ref=ref):
                    block_copy(ref, code & 31, out.at[pl.ds(offset, BLK)], sems.at[target, n]).start()

            return carry

        lax.fori_loop(0, jnp.minimum(asked[0, ROOM], ROOM), start, 0)

    for target, out in enumerate(outs):
        asked = lists[target]

        def wait(n, carry, target=target, out=out):
            block_copy(pieces[0], 0, out.at[pl.ds(0, BLK)], sems.at[target, n]).wait()
            return carry

        lax.fori_loop(0, jnp.minimum(asked[0, ROOM], ROOM), wait, 0)


def pack(here, lists, pieces):
    shape = jax.ShapeDtypeStruct((ROOM * BLK, BLK), jnp.bfloat16)
    return pl.pallas_call(
        pack_kernel,
        out_shape=(shape,) * 3,
        in_specs=[SMEM] * 4 + [ANY] * 4,
        out_specs=(ANY,) * 3,
        scratch_shapes=[pltpu.SemaphoreType.DMA((3, ROOM))],
    )(here, *lists, *pieces)


def local(block_values, block_columns, pattern_columns):
    row, depth, z = lax.axis_index("row"), lax.axis_index("depth"), lax.axis_index("col")
    here = jnp.stack([row % 2, row // 2 * 2 + depth % 2, depth // 2, z]).astype(jnp.int32)
    own_pattern = lax.dynamic_slice_in_dim(pattern_columns, depth * ROWS, ROWS, 0)

    piece = block_values.reshape(LEFT * BLK, BLK)
    left = lax.all_gather(piece, "col", axis=0, tiled=True)
    near = jnp.concatenate(first_pieces(piece), axis=0)

    marks = jnp.concatenate([block_columns.reshape(1, -1), own_pattern.reshape(1, -1)], axis=1)
    marks = jnp.pad(marks, ((0, 0), (0, BLK - marks.shape[1])))
    row_marks, plane_marks = doubled(marks, 1, along_z), doubled(marks, 1, along_x)
    row_marks, plane_marks = doubled(row_marks, 2, along_z), doubled(plane_marks, 2, along_x)
    row_marks, plane_marks, near = lax.optimization_barrier((row_marks, plane_marks, near))
    row_marks, plane_marks = doubled(row_marks, 4, along_z), doubled(plane_marks, 1, along_y)
    plane_marks = doubled(plane_marks, 2, along_y)
    plus, minus, other_marks = second_ring(near, 1), second_ring(near, -1), swap(row_marks)
    plus, minus, row_marks, other_marks, plane_marks = lax.optimization_barrier(
        (plus, minus, row_marks, other_marks, plane_marks)
    )
    far = far_pieces(plus, minus)
    left, near, plus, minus = lax.optimization_barrier((left, near, plus, minus))
    right = (near, plus, minus) + far
    x_jobs, s_jobs, takes = plan(here, row_marks, other_marks, plane_marks)
    left_other = swap(left)

    add = lambda mine, theirs: mine + swap(theirs).astype(jnp.float32)
    square = add(*product(x_jobs, left, left_other, right, False)).astype(jnp.bfloat16)
    square, takes = lax.optimization_barrier((square, takes))
    pieces = first_pieces(square)
    asked = tuple(second_ring(takes[index : index + 1], step) for index, step in ((1, -1), (2, 1), (3, 2)))
    most = functools.reduce(jnp.maximum, asked, takes[:1])[0, ROOM + 1]

    def packed(pieces):
        sent = pack(here, asked, pieces)
        got = tuple(second_ring(part, step) for part, step in zip(sent, (1, -1, 2)))
        return tuple(product(s_jobs, left, left_other, pieces + got, True))

    def dense(pieces):
        near = jnp.concatenate(pieces, axis=0)
        plus, minus = second_ring(near, 1), second_ring(near, -1)
        return tuple(product(s_jobs, left, left_other, (near, plus, minus) + far_pieces(plus, minus), False))

    cube = add(*lax.cond(most <= ROOM, packed, dense, pieces)).reshape(ROWS, KC, BLK, BLK)
    stored = jnp.where((block_columns >= 0)[:, :, None, None], block_values, 0).astype(jnp.float32)
    mapped = jnp.pad(stored, ((0, 0), (0, KC - KA), (0, 0), (0, 0)))
    return (1.5 * mapped - 0.5 * cube).astype(jnp.bfloat16)


def solution(mesh):
    placed = (P(("row", "depth"), "col", None, None), P(("row", "depth"), "col"), P("row", "col"))
    return jax.shard_map(
        local,
        mesh=mesh,
        in_specs=placed,
        out_specs=P(("row", "depth"), "col", None, None),
        check_vma=False,
    )
```

```python
import functools

import jax
import jax.numpy as jnp
from jax import lax
from jax.experimental import pallas as pl
from jax.experimental.pallas import tpu as pltpu
from jax.sharding import PartitionSpec as P

BLK = 128
KA = 2
KC = 3
TP = 24
ROWS = 6
OUTS = ROWS * KC
LEFT = ROWS * KA
ROOM = 22
COUNT, MOST = 32, 33
PAY = LEFT * BLK + 16
UNIT = 16
SLOTS = 64
JOBS = 2 * ROWS * 8 * KC
ALL = ("row", "col", "depth")


def chip_of(device):
    row, col, depth = device // 64, device // 8 % 8, device % 8
    return row // 2 * 2 + depth % 2, depth // 2, col, row % 2


def device_of(x, y, z, core):
    return (x // 2 * 2 + core) * 64 + z * 8 + y * 2 + x % 2


def move(array, rule):
    pairs = []
    for device in range(256):
        x, y, z, core = rule(*chip_of(device))
        pairs.append((device, device_of(x % 4, y % 4, z % 8, core)))
    return lax.ppermute(array, ALL, pairs)


def first_ring(array, step):
    return move(array, lambda x, y, z, core: (x + step * (1 - core), y + step * core, z, core))


def second_ring(array, step):
    return move(array, lambda x, y, z, core: (x + step * core, y + step * (1 - core), z, core))


def swap(array):
    return move(array, lambda x, y, z, core: (x, y, z, 1 - core))


def ring_order(away):
    away = away & 3
    return jnp.where(away == 2, 3, jnp.where(away == 3, 2, away))


def first_pieces(piece):
    far, plus, minus = [first_ring(piece, step) for step in (2, 1, -1)]
    return piece, plus, minus, far


def far_pieces(plus, minus):
    half = plus.shape[0] // 2
    return second_ring(plus[:half], 1), second_ring(minus[half:], -1)


def block_copy(ref, unit, target, sem):
    offset = pl.multiple_of(unit * UNIT, UNIT)
    return pltpu.make_async_copy(ref.at[pl.ds(offset, BLK)], target, sem)


def plan_groups(here_ref, which, group_code):
    core, x, y = here_ref[0] ^ which, here_ref[1], here_ref[2]
    first, second = jnp.where(core == 0, x, y), jnp.where(core == 0, y, x)
    for group in range(16):
        at_x, at_y = group // 8 * 2 + group % 2, group // 4 % 2 * 2 + group // 2 % 2
        far = jnp.where(core == 0, at_x, at_y)
        group_code[0, which * 16 + group] = ring_order(first - far)
        group_code[1, which * 16 + group] = ring_order(second - jnp.where(core == 0, at_y, at_x))
        group_code[2, which * 16 + group] = far


def plan_scan(marks_ref, z, panels, plane_ref, group_code, slots, add):
    def scan_row(row, carry):
        wanted = [marks_ref[z, LEFT + row * KC + u] for u in range(KC)]
        for panel, base in panels:
            for side in range(KA):
                column = marks_ref[panel, row * KA + side]

                @pl.when(column >= 0)
                def _(panel=panel, base=base, side=side, column=column):
                    quarter = (column * 43) >> 8
                    place = column - quarter * ROWS
                    group = base + quarter
                    inner, outer = group_code[0, group], group_code[1, group]
                    table = (group & 16) + outer * 4 + inner
                    founds = []
                    for slot in range(slots):
                        start = place * KA if slots == KA else LEFT + place * KC
                        have = plane_ref[table, start + slot]
                        found = jnp.where(have == wanted[0], 0, jnp.where(have == wanted[1], 1, 2))
                        founds.append(jnp.where((found < 2) | (have == wanted[2]), found, -1))

                    @pl.when(functools.reduce(jnp.maximum, founds) >= 0)
                    def _():
                        left = (panel * LEFT + row * KA + side) * (BLK // UNIT)
                        for slot, found in enumerate(founds):
                            out = row * KC + found
                            pl.when(found >= 0)(functools.partial(add, group, inner, outer, place, slot, left, out))

        return carry

    lax.fori_loop(0, ROWS, scan_row, 0)


def plan_x_kernel(here_ref, own_ref, plane_ref, jobs, group_code):
    core, z = here_ref[0], here_ref[3]
    plan_groups(here_ref, 0, group_code)
    plan_groups(here_ref, 1, group_code)
    jobs[0] = 0

    def add(group, inner, outer, place, slot, left, out):
        count = jobs[0]
        jobs[0] = count + 1
        jobs[1 + count] = (left << 6) | out
        source = jnp.where(outer < 3, outer, 3 + (inner >> 1)) + jnp.where(group >= 16, 5, 0)
        ahead = jnp.where(outer < 3, inner, inner & 1) * (PAY // UNIT)
        jobs[1 + JOBS + count] = (source << 10) | (ahead + (place * KA + slot) * (BLK // UNIT))

    panels = [(panel, ((panel // 2 % 2) ^ core) * 16 + (panel // 4 * 2 + panel % 2) * 4) for panel in range(8)]
    plan_scan(own_ref, z, panels, plane_ref, group_code, KA, add)


def plan_s_kernel(here_ref, own_ref, other_ref, plane_ref, jobs, takes, seen, group_code):
    core, z = here_ref[0], here_ref[3]
    plan_groups(here_ref, 0, group_code)
    jobs[0] = 0
    for outer in range(4):
        takes[outer, COUNT] = 0

    def clear(n, carry):
        seen[n] = -1
        return carry

    lax.fori_loop(0, 16 * OUTS, clear, 0, unroll=16)

    def add(half, group, inner, outer, place, slot, left, out):
        block = place * KC + slot
        mark = group * OUTS + block

        @pl.when((outer > 0) & (seen[mark] < 0))
        def _():
            rank = takes[outer, COUNT]
            takes[outer, COUNT] = rank + 1
            seen[mark] = rank

            @pl.when(rank < ROOM)
            def _():
                takes[outer, rank] = (group_code[2, group] << 5) | block

        count = jobs[0]
        jobs[0] = count + 1
        jobs[1 + count] = ((half * 8 * LEFT * (BLK // UNIT) + left) << 6) | (half * OUTS + out)
        near = (inner << 10) | (block * (BLK // UNIT))
        packed = ((3 + outer) << 10) | ((seen[mark] & 31) * (BLK // UNIT))
        dense = ((6 + outer) << 10) | ((inner * OUTS + block) * (BLK // UNIT))
        jobs[1 + JOBS + count] = jnp.where(outer == 0, near, packed)
        jobs[1 + 2 * JOBS + count] = jnp.where(outer == 0, near, dense)

    panels = [(panel // 2 * 4 + 2 * core + panel % 2, panel * 4) for panel in range(4)]
    for half, marks_ref in enumerate((own_ref, other_ref)):
        plan_scan(marks_ref, z, panels, plane_ref, group_code, KC, functools.partial(add, half))
    most = jnp.maximum(takes[1, COUNT], jnp.maximum(takes[2, COUNT], takes[3, COUNT]))
    for outer in range(4):
        takes[outer, MOST] = most


SMEM = pl.BlockSpec(memory_space=pltpu.SMEM)
VMEM = pl.BlockSpec(memory_space=pltpu.VMEM)
ANY = pl.BlockSpec(memory_space=pl.ANY)


JOB_TABLE = jax.ShapeDtypeStruct((1 + 3 * JOBS,), jnp.int32)


def plan_x(here, own, plane):
    return pl.pallas_call(
        plan_x_kernel,
        out_shape=JOB_TABLE,
        in_specs=[SMEM] * 3,
        out_specs=SMEM,
        scratch_shapes=[pltpu.SMEM((3, 32), jnp.int32)],
    )(here, own, plane)


def plan_s(here, own, other, plane):
    return pl.pallas_call(
        plan_s_kernel,
        out_shape=(JOB_TABLE, jax.ShapeDtypeStruct((4, BLK), jnp.int32)),
        in_specs=[SMEM] * 4,
        out_specs=(SMEM, SMEM),
        scratch_shapes=[pltpu.SMEM((16 * OUTS,), jnp.int32), pltpu.SMEM((3, 16), jnp.int32)],
    )(here, own, other, plane)


def product_kernel(lefts, rights, most_ref, jobs_ref, *refs):
    left_refs, right_refs, refs = refs[:lefts], refs[lefts : lefts + rights], refs[lefts + rights :]
    outs_refs, (total, left_buf, right_buf, sems) = refs[:lefts], refs[lefts:]
    count = jobs_ref[0]
    codes = jnp.where(most_ref[0] <= ROOM, 1 + JOBS, 1 + 2 * JOBS)

    def start(n):
        slot = n & (SLOTS - 1)
        left = jobs_ref[1 + n] >> 6
        code = jobs_ref[codes + n]
        source, unit = code >> 10, code & 1023
        whole = 8 * LEFT * (BLK // UNIT)
        for index, ref in enumerate(left_refs):

            @pl.when((left >= index * whole) & (left < (index + 1) * whole))
            def _(ref=ref, index=index):
                block_copy(ref, left - index * whole, left_buf.at[slot], sems.at[0, slot]).start()

        def right(low, high):
            if high - low == 1:
                block_copy(right_refs[low], unit, right_buf.at[slot], sems.at[1, slot]).start()
            else:
                middle = (low + high) // 2
                pl.when(source < middle)(functools.partial(right, low, middle))
                pl.when(source >= middle)(functools.partial(right, middle, high))

        right(0, rights)

    def wait(n):
        slot = n & (SLOTS - 1)
        block_copy(left_refs[0], 0, left_buf.at[slot], sems.at[0, slot]).wait()
        block_copy(left_refs[0], 0, right_buf.at[slot], sems.at[1, slot]).wait()

    def first(n, carry):
        start(n)
        return carry

    lax.fori_loop(0, jnp.minimum(count, SLOTS), first, 0)
    total[...] = jnp.zeros_like(total)

    def multiply(group, carry):
        at = [group * 4 + index for index in range(4)]
        for n in at:
            pl.when(n < count)(functools.partial(wait, n))
        outs = [jnp.where(n < count, jobs_ref[jnp.minimum(1 + n, JOBS)] & 63, lefts * OUTS) for n in at]
        slots = [n & (SLOTS - 1) for n in at]
        dots = [jnp.dot(left_buf[slot], right_buf[slot], preferred_element_type=jnp.float32) for slot in slots]
        for out, dot in zip(outs, dots):
            total[out] += dot
        for n in at:
            pl.when(n + SLOTS < count)(functools.partial(start, n + SLOTS))
        return carry

    lax.fori_loop(0, (count + 3) // 4, multiply, 0)
    for half, ref in enumerate(outs_refs):
        for block in range(OUTS):
            ref[pl.ds(block * BLK, BLK), :] = total[half * OUTS + block].astype(jnp.bfloat16)


def product(most, jobs, lefts, rights):
    return pl.pallas_call(
        functools.partial(product_kernel, len(lefts), len(rights)),
        out_shape=(jax.ShapeDtypeStruct((OUTS * BLK, BLK), jnp.bfloat16),) * len(lefts),
        in_specs=[SMEM] * 2 + [ANY] * (len(lefts) + len(rights)),
        out_specs=(VMEM,) * len(lefts),
        scratch_shapes=[
            pltpu.VMEM((len(lefts) * OUTS + 1, BLK, BLK), jnp.float32),
            pltpu.VMEM((SLOTS, BLK, BLK), jnp.bfloat16),
            pltpu.VMEM((SLOTS, BLK, BLK), jnp.bfloat16),
            pltpu.SemaphoreType.DMA((2, SLOTS)),
        ],
        compiler_params=pltpu.CompilerParams(vmem_limit_bytes=24 * 1024 * 1024),
    )(most, jobs, *lefts, *rights)


def pack_kernel(here_ref, *refs):
    lists, pieces, outs, sems = refs[:3], refs[3:7], refs[7:10], refs[10]
    first = jnp.where(here_ref[0] == 0, here_ref[1], here_ref[2])

    for target, (asked, out) in enumerate(zip(lists, outs)):

        def start(n, carry, target=target, out=out, asked=asked):
            code = asked[0, n]
            inner = ring_order(first - (code >> 5))
            offset = pl.multiple_of(n * BLK, BLK)
            for index, ref in enumerate(pieces):

                @pl.when(inner == index)
                def _(ref=ref):
                    block_copy(ref, (code & 31) * (BLK // UNIT), out.at[pl.ds(offset, BLK)], sems.at[target, n]).start()

            return carry

        lax.fori_loop(0, jnp.minimum(asked[0, COUNT], ROOM), start, 0)

    for target, (asked, out) in enumerate(zip(lists, outs)):

        def wait(n, carry, target=target, out=out):
            block_copy(pieces[0], 0, out.at[pl.ds(0, BLK)], sems.at[target, n]).wait()
            return carry

        lax.fori_loop(0, jnp.minimum(asked[0, COUNT], ROOM), wait, 0)


def pack(here, lists, pieces):
    shape = jax.ShapeDtypeStruct((ROOM * BLK, BLK), jnp.bfloat16)
    return pl.pallas_call(
        pack_kernel,
        out_shape=(shape,) * 3,
        in_specs=[SMEM] * 4 + [ANY] * 4,
        out_specs=(VMEM,) * 3,
        scratch_shapes=[pltpu.SemaphoreType.DMA((3, ROOM))],
    )(here, *lists, *pieces)


def blank(rows):
    shape = jax.ShapeDtypeStruct((rows, BLK), jnp.bfloat16)
    return tuple(pl.pallas_call(lambda *refs: None, out_shape=(shape,) * 3, out_specs=(ANY,) * 3)())


def second_pieces(most, here, lists, pieces):
    steps = (1, -1, 2)

    def packed(pieces):
        sent = pack(here, lists, pieces)
        return tuple(second_ring(part, step) for part, step in zip(sent, steps)) + blank(4 * OUTS * BLK)

    def dense(pieces):
        near = jnp.concatenate(pieces, axis=0)
        return blank(ROOM * BLK) + tuple(second_ring(near, step) for step in steps)

    return pieces + lax.cond(most[0] <= ROOM, packed, dense, pieces)


def marks_of(array):
    return array.reshape(-1, PAY, BLK)[:, LEFT * BLK, :].astype(jnp.int32)


def local(block_values, block_columns, pattern_columns):
    row, depth, z = lax.axis_index("row"), lax.axis_index("depth"), lax.axis_index("col")
    here = jnp.stack([row % 2, row // 2 * 2 + depth % 2, depth // 2, z]).astype(jnp.int32)
    own_pattern = lax.dynamic_slice_in_dim(pattern_columns, depth * ROWS, ROWS, 0)

    marks = jnp.concatenate([block_columns.reshape(1, -1), own_pattern.reshape(1, -1)], axis=1)
    marks = jnp.pad(marks.astype(jnp.bfloat16), ((0, 15), (0, BLK - marks.shape[1])))
    values = block_values.reshape(LEFT * BLK, BLK)
    left = lax.all_gather(values, "col", axis=0, tiled=True)
    piece = lax.optimization_barrier(jnp.concatenate([values, marks], axis=0))

    near = jnp.concatenate(first_pieces(piece), axis=0)
    near, marks = lax.optimization_barrier((near, marks[:1].astype(jnp.int32)))
    near_marks = marks_of(near)
    plus, minus, far_marks = second_ring(near, 1), second_ring(near, -1), second_ring(near_marks, 2)
    row_marks = lax.all_gather(marks, "col", axis=0, tiled=True)
    plus, minus, far_marks, row_marks = lax.optimization_barrier((plus, minus, far_marks, row_marks))
    other_marks = swap(row_marks)
    far = far_pieces(plus, minus)
    plane_marks = jnp.concatenate([near_marks, marks_of(plus), marks_of(minus), far_marks], axis=0)
    both_marks = jnp.concatenate([plane_marks, swap(plane_marks)], axis=0)
    x_jobs = plan_x(here, row_marks, both_marks)
    s_jobs, takes = plan_s(here, row_marks, other_marks, plane_marks)
    far, x_jobs, s_jobs = lax.optimization_barrier((far, x_jobs, s_jobs))
    right = (near, plus, minus) + far
    other_right = tuple(swap(part) for part in right)
    left, plus = lax.optimization_barrier((left, plus))

    zero = jnp.zeros((1,), jnp.int32)
    (square,) = product(zero, x_jobs, (left,), right + other_right)
    square, left = lax.optimization_barrier((square, left))
    first, *rest = first_pieces(square)
    left_other = swap(left)
    asked = tuple(second_ring(takes[index : index + 1], step) for index, step in ((1, -1), (2, 1), (3, 2)))
    most = functools.reduce(jnp.maximum, asked, takes[:1])[0, MOST:][:1]

    stored = jnp.where((block_columns >= 0)[:, :, None, None], block_values, 0).astype(jnp.float32)
    scaled = 1.5 * jnp.pad(stored, ((0, 0), (0, KC - KA), (0, 0), (0, 0))).reshape(OUTS * BLK, BLK)
    first, scaled = lax.optimization_barrier((first, scaled))

    s_right = second_pieces(most, here, asked, (first, *rest))
    mine, theirs = product(most, s_jobs, (left, left_other), s_right)
    cube = mine.astype(jnp.float32) + swap(theirs).astype(jnp.float32)
    return (scaled - 0.5 * cube).astype(jnp.bfloat16).reshape(ROWS, KC, BLK, BLK)


def solution(mesh):
    placed = (P(("row", "depth"), "col", None, None), P(("row", "depth"), "col"), P("row", "col"))
    return jax.shard_map(
        local,
        mesh=mesh,
        in_specs=placed,
        out_specs=P(("row", "depth"), "col", None, None),
        check_vma=False,
    )
```

```python
import functools

import jax
import jax.numpy as jnp
from jax import lax
from jax.experimental import pallas as pl
from jax.experimental.pallas import tpu as pltpu
from jax.sharding import PartitionSpec as P

BLK = 128
KA = 2
KC = 3
TP = 24
ROWS = 6
OUTS = ROWS * KC
LEFT = ROWS * KA
ROOM = 22
COUNT, MOST = 32, 33
PAY = LEFT * BLK + 16
UNIT = 16
SLOTS = 64
JOBS = 2 * ROWS * 8 * KC
ALL = ("row", "col", "depth")


def chip_of(device):
    row, col, depth = device // 64, device // 8 % 8, device % 8
    return row // 2 * 2 + depth % 2, depth // 2, col, row % 2


def device_of(x, y, z, core):
    return (x // 2 * 2 + core) * 64 + z * 8 + y * 2 + x % 2


def move(array, rule):
    pairs = []
    for device in range(256):
        x, y, z, core = rule(*chip_of(device))
        pairs.append((device, device_of(x % 4, y % 4, z % 8, core)))
    return lax.ppermute(array, ALL, pairs)


def first_ring(array, step):
    return move(array, lambda x, y, z, core: (x + step * (1 - core), y + step * core, z, core))


def second_ring(array, step):
    return move(array, lambda x, y, z, core: (x + step * core, y + step * (1 - core), z, core))


def swap(array):
    return move(array, lambda x, y, z, core: (x, y, z, 1 - core))


def ring_order(away):
    away = away & 3
    return jnp.where(away == 2, 3, jnp.where(away == 3, 2, away))


def first_pieces(piece):
    far, plus, minus = [first_ring(piece, step) for step in (2, 1, -1)]
    return piece, plus, minus, far


def block_copy(ref, unit, target, sem):
    offset = pl.multiple_of(unit * UNIT, UNIT)
    return pltpu.make_async_copy(ref.at[pl.ds(offset, BLK)], target, sem)


def plan_groups(here_ref, which, group_code):
    core, x, y = here_ref[0] ^ which, here_ref[1], here_ref[2]
    first, second = jnp.where(core == 0, x, y), jnp.where(core == 0, y, x)
    for group in range(16):
        at_x, at_y = group // 8 * 2 + group % 2, group // 4 % 2 * 2 + group // 2 % 2
        far = jnp.where(core == 0, at_x, at_y)
        inner = ring_order(first - far)
        outer = ring_order(second - jnp.where(core == 0, at_y, at_x))
        group_code[0, which * 16 + group] = inner
        group_code[1, which * 16 + group] = outer
        group_code[2, which * 16 + group] = far
        group_code[3, which * 16 + group] = outer * 4 + inner


def plan_scan(marks_ref, z, panels, plane_ref, group_code, slots, add):
    def look(row, panel, base, side, wanted):
        column = marks_ref[panel, row * KA + side]
        known = jnp.maximum(column, 0)
        quarter = (known * 43) >> 8
        place = known - quarter * ROWS
        group = base + quarter
        table = group_code[3, group]
        founds = []
        for slot in range(slots):
            start = place * KA + (group & 16) * 4 if slots == KA else LEFT + place * KC
            have = plane_ref[table, start + slot]
            found = jnp.where(have == wanted[0], 0, jnp.where(have == wanted[1], 1, 2))
            founds.append(jnp.where((found < 2) | (have == wanted[2]), found, -1))
        best = jnp.where(column >= 0, functools.reduce(jnp.maximum, founds), -1)
        return best, founds, group, place

    def scan_row(row, carry):
        wanted = [marks_ref[z, LEFT + row * KC + u] for u in range(KC)]
        entries = [(panel, base, side) for panel, base in panels for side in range(KA)]
        for first in range(0, len(entries), 4):
            some = entries[first : first + 4]
            for (panel, _, side), (best, founds, group, place) in zip(some, [look(row, *entry, wanted) for entry in some]):

                @pl.when(best >= 0)
                def _(panel=panel, side=side, founds=founds, group=group, place=place):
                    left = (panel * LEFT + row * KA + side) * (BLK // UNIT)
                    inner, outer = group_code[0, group], group_code[1, group]
                    for slot, found in enumerate(founds):
                        out = row * KC + found
                        pl.when(found >= 0)(functools.partial(add, group, inner, outer, place, slot, left, out))

        return carry

    lax.fori_loop(0, ROWS, scan_row, 0)


def plan_kernel(here_ref, own_ref, other_ref, plane_ref, x_jobs, s_jobs, takes, seen, group_code):
    core, z = here_ref[0], here_ref[3]
    plan_groups(here_ref, 0, group_code)
    plan_groups(here_ref, 1, group_code)
    x_jobs[0] = 0
    s_jobs[0] = 0
    for outer in range(4):
        takes[outer, COUNT] = 0

    def clear(n, carry):
        seen[n] = -1
        return carry

    lax.fori_loop(0, 16 * OUTS, clear, 0, unroll=16)

    def add_x(group, inner, outer, place, slot, left, out):
        count = x_jobs[0]
        x_jobs[0] = count + 1
        x_jobs[1 + count] = (left << 6) | out
        source = jnp.where(outer < 3, outer, 3 + (inner >> 1)) + jnp.where(group >= 16, 5, 0)
        ahead = jnp.where(outer < 3, inner, inner & 1) * (PAY // UNIT)
        x_jobs[1 + JOBS + count] = (source << 10) | (ahead + (place * KA + slot) * (BLK // UNIT))

    def add_s(half, group, inner, outer, place, slot, left, out):
        block = place * KC + slot
        mark = group * OUTS + block

        @pl.when((outer > 0) & (seen[mark] < 0))
        def _():
            rank = takes[outer, COUNT]
            takes[outer, COUNT] = rank + 1
            seen[mark] = rank

            @pl.when(rank < ROOM)
            def _():
                takes[outer, rank] = (group_code[2, group] << 5) | block

        count = s_jobs[0]
        s_jobs[0] = count + 1
        s_jobs[1 + count] = ((half * 8 * LEFT * (BLK // UNIT) + left) << 6) | (half * OUTS + out)
        near = (inner << 10) | (block * (BLK // UNIT))
        packed = ((3 + outer) << 10) | ((seen[mark] & 31) * (BLK // UNIT))
        dense = ((6 + outer) << 10) | ((inner * OUTS + block) * (BLK // UNIT))
        s_jobs[1 + JOBS + count] = jnp.where(outer == 0, near, packed)
        s_jobs[1 + 2 * JOBS + count] = jnp.where(outer == 0, near, dense)

    panels = [(panel, ((panel // 2 % 2) ^ core) * 16 + (panel // 4 * 2 + panel % 2) * 4) for panel in range(8)]
    plan_scan(own_ref, z, panels, plane_ref, group_code, KA, add_x)
    panels = [(panel // 2 * 4 + 2 * core + panel % 2, panel * 4) for panel in range(4)]
    for half, marks_ref in enumerate((own_ref, other_ref)):
        plan_scan(marks_ref, z, panels, plane_ref, group_code, KC, functools.partial(add_s, half))
    most = jnp.maximum(takes[1, COUNT], jnp.maximum(takes[2, COUNT], takes[3, COUNT]))
    for outer in range(4):
        takes[outer, MOST] = most


SMEM = pl.BlockSpec(memory_space=pltpu.SMEM)
VMEM = pl.BlockSpec(memory_space=pltpu.VMEM)
ANY = pl.BlockSpec(memory_space=pl.ANY)


SMALL = pl.CostEstimate(flops=1000, bytes_accessed=1000, transcendentals=0)
JOB_TABLE = jax.ShapeDtypeStruct((1 + 3 * JOBS,), jnp.int32)


def plan(here, own, other, plane):
    return pl.pallas_call(
        plan_kernel,
        out_shape=(JOB_TABLE, JOB_TABLE, jax.ShapeDtypeStruct((4, BLK), jnp.int32)),
        in_specs=[SMEM] * 4,
        out_specs=(SMEM,) * 3,
        scratch_shapes=[pltpu.SMEM((16 * OUTS,), jnp.int32), pltpu.SMEM((4, 32), jnp.int32)],
        cost_estimate=SMALL,
    )(here, own, other, plane)


def product_kernel(lefts, rights, most_ref, jobs_ref, *refs):
    left_refs, right_refs, refs = refs[:lefts], refs[lefts : lefts + rights], refs[lefts + rights :]
    outs_refs, (total, left_buf, right_buf, sems) = refs[:lefts], refs[lefts:]
    count = jobs_ref[0]
    codes = jnp.where(most_ref[0] <= ROOM, 1 + JOBS, 1 + 2 * JOBS)

    def start(n):
        slot = n & (SLOTS - 1)
        left = jobs_ref[1 + n] >> 6
        code = jobs_ref[codes + n]
        source, unit = code >> 10, code & 1023
        whole = 8 * LEFT * (BLK // UNIT)
        for index, ref in enumerate(left_refs):

            @pl.when((left >= index * whole) & (left < (index + 1) * whole))
            def _(ref=ref, index=index):
                block_copy(ref, left - index * whole, left_buf.at[slot], sems.at[0, slot]).start()

        def right(low, high):
            if high - low == 1:
                block_copy(right_refs[low], unit, right_buf.at[slot], sems.at[1, slot]).start()
            else:
                middle = (low + high) // 2
                pl.when(source < middle)(functools.partial(right, low, middle))
                pl.when(source >= middle)(functools.partial(right, middle, high))

        right(0, rights)

    def wait(n):
        slot = n & (SLOTS - 1)
        block_copy(left_refs[0], 0, left_buf.at[slot], sems.at[0, slot]).wait()
        block_copy(left_refs[0], 0, right_buf.at[slot], sems.at[1, slot]).wait()

    def first(n, carry):
        start(n)
        return carry

    lax.fori_loop(0, jnp.minimum(count, SLOTS), first, 0)
    total[...] = jnp.zeros_like(total)

    def multiply(group, carry):
        at = [group * 4 + index for index in range(4)]
        for n in at:
            pl.when(n < count)(functools.partial(wait, n))
        outs = [jnp.where(n < count, jobs_ref[jnp.minimum(1 + n, JOBS)] & 63, lefts * OUTS) for n in at]
        slots = [n & (SLOTS - 1) for n in at]
        dots = [jnp.dot(left_buf[slot], right_buf[slot], preferred_element_type=jnp.float32) for slot in slots]
        for out, dot in zip(outs, dots):
            total[out] += dot
        for n in at:
            pl.when(n + SLOTS < count)(functools.partial(start, n + SLOTS))
        return carry

    lax.fori_loop(0, (count + 3) // 4, multiply, 0)
    for half, ref in enumerate(outs_refs):
        for block in range(OUTS):
            ref[pl.ds(block * BLK, BLK), :] = total[half * OUTS + block].astype(jnp.bfloat16)


def product(most, jobs, lefts, rights):
    return pl.pallas_call(
        functools.partial(product_kernel, len(lefts), len(rights)),
        out_shape=(jax.ShapeDtypeStruct((OUTS * BLK, BLK), jnp.bfloat16),) * len(lefts),
        in_specs=[SMEM] * 2 + [ANY] * (len(lefts) + len(rights)),
        out_specs=(VMEM,) * len(lefts),
        scratch_shapes=[
            pltpu.VMEM((len(lefts) * OUTS + 1, BLK, BLK), jnp.float32),
            pltpu.VMEM((SLOTS, BLK, BLK), jnp.bfloat16),
            pltpu.VMEM((SLOTS, BLK, BLK), jnp.bfloat16),
            pltpu.SemaphoreType.DMA((2, SLOTS)),
        ],
        compiler_params=pltpu.CompilerParams(vmem_limit_bytes=10 * 1024 * 1024),
    )(most, jobs, *lefts, *rights)


def pack_kernel(here_ref, *refs):
    lists, pieces, outs, sems = refs[:3], refs[3:7], refs[7:10], refs[10]
    first = jnp.where(here_ref[0] == 0, here_ref[1], here_ref[2])

    for target, (asked, out) in enumerate(zip(lists, outs)):

        def start(n, carry, target=target, out=out, asked=asked):
            code = asked[0, n]
            inner = ring_order(first - (code >> 5))
            offset = pl.multiple_of(n * BLK, BLK)
            for index, ref in enumerate(pieces):

                @pl.when(inner == index)
                def _(ref=ref):
                    block_copy(ref, (code & 31) * (BLK // UNIT), out.at[pl.ds(offset, BLK)], sems.at[target, n]).start()

            return carry

        lax.fori_loop(0, jnp.minimum(asked[0, COUNT], ROOM), start, 0)

    for target, (asked, out) in enumerate(zip(lists, outs)):

        def wait(n, carry, target=target, out=out):
            block_copy(pieces[0], 0, out.at[pl.ds(0, BLK)], sems.at[target, n]).wait()
            return carry

        lax.fori_loop(0, jnp.minimum(asked[0, COUNT], ROOM), wait, 0)


def pack(here, lists, pieces):
    shape = jax.ShapeDtypeStruct((ROOM * BLK, BLK), jnp.bfloat16)
    return pl.pallas_call(
        pack_kernel,
        out_shape=(shape,) * 3,
        in_specs=[SMEM] * 4 + [ANY] * 4,
        out_specs=(VMEM,) * 3,
        scratch_shapes=[pltpu.SemaphoreType.DMA((3, ROOM))],
    )(here, *lists, *pieces)


def blank(rows):
    shape = jax.ShapeDtypeStruct((rows, BLK), jnp.bfloat16)
    return tuple(pl.pallas_call(lambda *refs: None, out_shape=(shape,) * 3, out_specs=(ANY,) * 3)())


def second_pieces(most, here, lists, pieces):
    steps = (1, -1, 2)

    def packed(pieces):
        sent = pack(here, lists, pieces)
        return tuple(second_ring(part, step) for part, step in zip(sent, steps)) + blank(4 * OUTS * BLK)

    def dense(pieces):
        near = jnp.concatenate(pieces, axis=0)
        return blank(ROOM * BLK) + tuple(second_ring(near, step) for step in steps)

    return pieces + lax.cond(most[0] <= ROOM, packed, dense, pieces)


def marks_of(array):
    return array.reshape(-1, PAY, BLK)[:, LEFT * BLK, :].astype(jnp.int32)


def local(block_values, block_columns, pattern_columns):
    row, depth, z = lax.axis_index("row"), lax.axis_index("depth"), lax.axis_index("col")
    here = jnp.stack([row % 2, row // 2 * 2 + depth % 2, depth // 2, z]).astype(jnp.int32)
    own_pattern = lax.dynamic_slice_in_dim(pattern_columns, depth * ROWS, ROWS, 0)

    marks = jnp.concatenate([block_columns.reshape(1, -1), own_pattern.reshape(1, -1)], axis=1)
    marks = jnp.pad(marks.astype(jnp.bfloat16), ((0, 15), (0, BLK - marks.shape[1])))
    values = block_values.reshape(LEFT * BLK, BLK)
    left = lax.all_gather(values, "col", axis=0, tiled=True)
    piece = lax.optimization_barrier(jnp.concatenate([values, marks], axis=0))

    near = jnp.concatenate(first_pieces(piece), axis=0)
    near, marks = lax.optimization_barrier((near, marks[:1].astype(jnp.int32)))
    near_marks = marks_of(near)
    plus, minus, far_marks = second_ring(near, 1), second_ring(near, -1), second_ring(near_marks, 2)
    row_marks = lax.all_gather(marks, "col", axis=0, tiled=True)
    plus, minus, far_marks, row_marks = lax.optimization_barrier((plus, minus, far_marks, row_marks))
    half = plus.shape[0] // 2
    far = second_ring(plus[:half], 1), second_ring(minus[half:], -1)
    plane_marks = jnp.concatenate([near_marks, marks_of(plus), marks_of(minus), far_marks], axis=0)
    beside = jnp.pad(swap(plane_marks)[:, : BLK // 2], ((0, 0), (BLK // 2, 0)))
    x_jobs, s_jobs, takes = plan(here, row_marks, swap(row_marks), plane_marks + beside)
    far, x_jobs = lax.optimization_barrier((far, x_jobs))
    right = (near, plus, minus) + far
    other_right = tuple(swap(part) for part in right)
    left, x_jobs = lax.optimization_barrier((left, x_jobs))

    zero = jnp.zeros((1,), jnp.int32)
    (square,) = product(zero, x_jobs, (left,), right + other_right)
    square, left = lax.optimization_barrier((square, left))
    first, *rest = first_pieces(square)
    left_other = swap(left)
    asked = tuple(second_ring(takes[index : index + 1], step) for index, step in ((1, -1), (2, 1), (3, 2)))
    most = functools.reduce(jnp.maximum, asked, takes[:1])[0, MOST:][:1]

    stored = jnp.where((block_columns >= 0)[:, :, None, None], block_values, 0).astype(jnp.float32)
    scaled = 1.5 * jnp.pad(stored, ((0, 0), (0, KC - KA), (0, 0), (0, 0))).reshape(OUTS * BLK, BLK)
    first, scaled = lax.optimization_barrier((first, scaled))

    s_right = second_pieces(most, here, asked, (first, *rest))
    mine, theirs = product(most, s_jobs, (left, left_other), s_right)
    cube = mine.astype(jnp.float32) + swap(theirs).astype(jnp.float32)
    return (scaled - 0.5 * cube).astype(jnp.bfloat16).reshape(ROWS, KC, BLK, BLK)


def solution(mesh):
    placed = (P(("row", "depth"), "col", None, None), P(("row", "depth"), "col"), P("row", "col"))
    return jax.shard_map(
        local,
        mesh=mesh,
        in_specs=placed,
        out_specs=P(("row", "depth"), "col", None, None),
        check_vma=False,
    )
```

```python
import functools

import jax
import jax.numpy as jnp
from jax import lax
from jax.experimental import pallas as pl
from jax.experimental.pallas import tpu as pltpu
from jax.sharding import PartitionSpec as P

BLK = 128
KA = 2
KC = 3
TP = 24
ROWS = 6
OUTS = ROWS * KC
LEFT = ROWS * KA
ROOM = 22
COUNT, MOST = 32, 33
PAY = LEFT * BLK + 16
UNIT = 16
SLOTS = 64
JOBS = 2 * ROWS * 8 * KC
ALL = ("row", "col", "depth")


def chip_of(device):
    row, col, depth = device // 64, device // 8 % 8, device % 8
    return row // 2 * 2 + depth % 2, depth // 2, col, row % 2


def device_of(x, y, z, core):
    return (x // 2 * 2 + core) * 64 + z * 8 + y * 2 + x % 2


def move(array, rule):
    pairs = []
    for device in range(256):
        x, y, z, core = rule(*chip_of(device))
        pairs.append((device, device_of(x % 4, y % 4, z % 8, core)))
    return lax.ppermute(array, ALL, pairs)


def first_ring(array, step):
    return move(array, lambda x, y, z, core: (x + step * (1 - core), y + step * core, z, core))


def second_ring(array, step):
    return move(array, lambda x, y, z, core: (x + step * core, y + step * (1 - core), z, core))


def swap(array):
    return move(array, lambda x, y, z, core: (x, y, z, 1 - core))


def ring_order(away):
    away = away & 3
    return jnp.where(away == 2, 3, jnp.where(away == 3, 2, away))


def first_pieces(piece):
    far, plus, minus = [first_ring(piece, step) for step in (2, 1, -1)]
    return piece, plus, minus, far


def block_copy(ref, unit, target, sem):
    offset = pl.multiple_of(unit * UNIT, UNIT)
    return pltpu.make_async_copy(ref.at[pl.ds(offset, BLK)], target, sem)


def plan_groups(here_ref, which, group_code):
    core, x, y = here_ref[0] ^ which, here_ref[1], here_ref[2]
    first, second = jnp.where(core == 0, x, y), jnp.where(core == 0, y, x)
    for group in range(16):
        at_x, at_y = group // 8 * 2 + group % 2, group // 4 % 2 * 2 + group // 2 % 2
        far = jnp.where(core == 0, at_x, at_y)
        inner = ring_order(first - far)
        outer = ring_order(second - jnp.where(core == 0, at_y, at_x))
        group_code[0, which * 16 + group] = inner
        group_code[1, which * 16 + group] = outer
        group_code[2, which * 16 + group] = far
        group_code[3, which * 16 + group] = outer * 4 + inner


def plan_scan(marks_ref, z, panels, plane_ref, group_code, slots, add):
    def look(row, panel, base, side, wanted):
        column = marks_ref[panel, row * KA + side]
        known = jnp.maximum(column, 0)
        quarter = (known * 43) >> 8
        place = known - quarter * ROWS
        group = base + quarter
        table = group_code[3, group]
        founds = []
        for slot in range(slots):
            start = place * KA + (group & 16) * 4 if slots == KA else LEFT + place * KC
            have = plane_ref[table, start + slot]
            found = jnp.where(have == wanted[0], 0, jnp.where(have == wanted[1], 1, 2))
            founds.append(jnp.where((found < 2) | (have == wanted[2]), found, -1))
        best = jnp.where(column >= 0, functools.reduce(jnp.maximum, founds), -1)
        return best, founds, group, place

    def scan_row(row, carry):
        wanted = [marks_ref[z, LEFT + row * KC + u] for u in range(KC)]
        entries = [(panel, base, side) for panel, base in panels for side in range(KA)]
        for first in range(0, len(entries), 4):
            some = entries[first : first + 4]
            for (panel, _, side), (best, founds, group, place) in zip(some, [look(row, *entry, wanted) for entry in some]):

                @pl.when(best >= 0)
                def _(panel=panel, side=side, founds=founds, group=group, place=place):
                    left = (panel * LEFT + row * KA + side) * (BLK // UNIT)
                    inner, outer = group_code[0, group], group_code[1, group]
                    for slot, found in enumerate(founds):
                        out = row * KC + found
                        pl.when(found >= 0)(functools.partial(add, group, inner, outer, place, slot, left, out))

        return carry

    lax.fori_loop(0, ROWS, scan_row, 0)


def plan_kernel(here_ref, own_ref, other_ref, plane_ref, x_jobs, s_jobs, takes, seen, group_code):
    core, z = here_ref[0], here_ref[3]
    plan_groups(here_ref, 0, group_code)
    plan_groups(here_ref, 1, group_code)
    x_jobs[0] = 0
    s_jobs[0] = 0
    for outer in range(4):
        takes[outer, COUNT] = 0

    def clear(n, carry):
        seen[n] = -1
        return carry

    lax.fori_loop(0, 16 * OUTS, clear, 0, unroll=16)

    def add_x(group, inner, outer, place, slot, left, out):
        count = x_jobs[0]
        x_jobs[0] = count + 1
        x_jobs[1 + count] = (left << 6) | out
        source = jnp.where(outer < 3, outer, 3 + (inner >> 1)) + jnp.where(group >= 16, 5, 0)
        ahead = jnp.where(outer < 3, inner, inner & 1) * (PAY // UNIT)
        x_jobs[1 + JOBS + count] = (source << 10) | (ahead + (place * KA + slot) * (BLK // UNIT))

    def add_s(half, group, inner, outer, place, slot, left, out):
        block = place * KC + slot
        mark = group * OUTS + block

        @pl.when((outer > 0) & (seen[mark] < 0))
        def _():
            rank = takes[outer, COUNT]
            takes[outer, COUNT] = rank + 1
            seen[mark] = rank

            @pl.when(rank < ROOM)
            def _():
                takes[outer, rank] = (group_code[2, group] << 5) | block

        count = s_jobs[0]
        s_jobs[0] = count + 1
        s_jobs[1 + count] = ((half * 8 * LEFT * (BLK // UNIT) + left) << 6) | (half * OUTS + out)
        near = (inner << 10) | (block * (BLK // UNIT))
        packed = ((3 + outer) << 10) | ((seen[mark] & 31) * (BLK // UNIT))
        dense = ((6 + outer) << 10) | ((inner * OUTS + block) * (BLK // UNIT))
        s_jobs[1 + JOBS + count] = jnp.where(outer == 0, near, packed)
        s_jobs[1 + 2 * JOBS + count] = jnp.where(outer == 0, near, dense)

    def add_both(group, inner, outer, place, slot, left, out):
        add_s(0, group, inner, outer, place, slot, left, out)
        if slot < KA:
            held = plane_ref[group_code[3, group], place * KA + slot] >= 0
            pl.when(held)(functools.partial(add_x, group, inner, outer, place, slot, left, out))

    panels = [(panel // 2 * 4 + 2 * core + panel % 2, panel * 4) for panel in range(4)]
    plan_scan(own_ref, z, panels, plane_ref, group_code, KC, add_both)
    plan_scan(other_ref, z, panels, plane_ref, group_code, KC, functools.partial(add_s, 1))
    panels = [(panel // 2 * 4 + 2 * (1 - core) + panel % 2, 16 + panel * 4) for panel in range(4)]
    plan_scan(own_ref, z, panels, plane_ref, group_code, KA, add_x)
    most = jnp.maximum(takes[1, COUNT], jnp.maximum(takes[2, COUNT], takes[3, COUNT]))
    for outer in range(4):
        takes[outer, MOST] = most


SMEM = pl.BlockSpec(memory_space=pltpu.SMEM)
VMEM = pl.BlockSpec(memory_space=pltpu.VMEM)
ANY = pl.BlockSpec(memory_space=pl.ANY)


SMALL = pl.CostEstimate(flops=1000, bytes_accessed=1000, transcendentals=0)
JOB_TABLE = jax.ShapeDtypeStruct((1 + 3 * JOBS,), jnp.int32)


def plan(here, own, other, plane):
    return pl.pallas_call(
        plan_kernel,
        out_shape=(JOB_TABLE, JOB_TABLE, jax.ShapeDtypeStruct((4, BLK), jnp.int32)),
        in_specs=[SMEM] * 4,
        out_specs=(SMEM,) * 3,
        scratch_shapes=[pltpu.SMEM((16 * OUTS,), jnp.int32), pltpu.SMEM((4, 32), jnp.int32)],
        cost_estimate=SMALL,
    )(here, own, other, plane)


def product_kernel(lefts, rights, most_ref, jobs_ref, *refs):
    left_refs, right_refs, refs = refs[:lefts], refs[lefts : lefts + rights], refs[lefts + rights :]
    outs_refs, (total, left_buf, right_buf, sems) = refs[:lefts], refs[lefts:]
    count = jobs_ref[0]
    codes = jnp.where(most_ref[0] <= ROOM, 1 + JOBS, 1 + 2 * JOBS)

    def start(n):
        slot = n & (SLOTS - 1)
        left = jobs_ref[1 + n] >> 6
        code = jobs_ref[codes + n]
        source, unit = code >> 10, code & 1023
        whole = 8 * LEFT * (BLK // UNIT)
        for index, ref in enumerate(left_refs):

            @pl.when((left >= index * whole) & (left < (index + 1) * whole))
            def _(ref=ref, index=index):
                block_copy(ref, left - index * whole, left_buf.at[slot], sems.at[0, slot]).start()

        def right(low, high):
            if high - low == 1:
                block_copy(right_refs[low], unit, right_buf.at[slot], sems.at[1, slot]).start()
            else:
                middle = (low + high) // 2
                pl.when(source < middle)(functools.partial(right, low, middle))
                pl.when(source >= middle)(functools.partial(right, middle, high))

        right(0, rights)

    def wait(n):
        slot = n & (SLOTS - 1)
        block_copy(left_refs[0], 0, left_buf.at[slot], sems.at[0, slot]).wait()
        block_copy(left_refs[0], 0, right_buf.at[slot], sems.at[1, slot]).wait()

    def first(n, carry):
        start(n)
        return carry

    lax.fori_loop(0, jnp.minimum(count, SLOTS), first, 0)
    total[...] = jnp.zeros_like(total)

    def multiply(group, carry):
        at = [group * 4 + index for index in range(4)]
        for n in at:
            pl.when(n < count)(functools.partial(wait, n))
        outs = [jnp.where(n < count, jobs_ref[jnp.minimum(1 + n, JOBS)] & 63, lefts * OUTS) for n in at]
        slots = [n & (SLOTS - 1) for n in at]
        dots = [jnp.dot(left_buf[slot], right_buf[slot], preferred_element_type=jnp.float32) for slot in slots]
        for out, dot in zip(outs, dots):
            total[out] += dot
        for n in at:
            pl.when(n + SLOTS < count)(functools.partial(start, n + SLOTS))
        return carry

    lax.fori_loop(0, (count + 3) // 4, multiply, 0)
    for half, ref in enumerate(outs_refs):
        for block in range(OUTS):
            ref[pl.ds(block * BLK, BLK), :] = total[half * OUTS + block].astype(jnp.bfloat16)


def product(most, jobs, lefts, rights):
    return pl.pallas_call(
        functools.partial(product_kernel, len(lefts), len(rights)),
        out_shape=(jax.ShapeDtypeStruct((OUTS * BLK, BLK), jnp.bfloat16),) * len(lefts),
        in_specs=[SMEM] * 2 + [ANY] * (len(lefts) + len(rights)),
        out_specs=(VMEM,) * len(lefts),
        scratch_shapes=[
            pltpu.VMEM((len(lefts) * OUTS + 1, BLK, BLK), jnp.float32),
            pltpu.VMEM((SLOTS, BLK, BLK), jnp.bfloat16),
            pltpu.VMEM((SLOTS, BLK, BLK), jnp.bfloat16),
            pltpu.SemaphoreType.DMA((2, SLOTS)),
        ],
        compiler_params=pltpu.CompilerParams(vmem_limit_bytes=10 * 1024 * 1024),
    )(most, jobs, *lefts, *rights)


def pack_kernel(here_ref, *refs):
    lists, pieces, outs, sems = refs[:3], refs[3:7], refs[7:10], refs[10]
    first = jnp.where(here_ref[0] == 0, here_ref[1], here_ref[2])

    for target, (asked, out) in enumerate(zip(lists, outs)):

        def start(n, carry, target=target, out=out, asked=asked):
            code = asked[0, n]
            inner = ring_order(first - (code >> 5))
            offset = pl.multiple_of(n * BLK, BLK)
            for index, ref in enumerate(pieces):

                @pl.when(inner == index)
                def _(ref=ref):
                    block_copy(ref, (code & 31) * (BLK // UNIT), out.at[pl.ds(offset, BLK)], sems.at[target, n]).start()

            return carry

        lax.fori_loop(0, jnp.minimum(asked[0, COUNT], ROOM), start, 0)

    for target, (asked, out) in enumerate(zip(lists, outs)):

        def wait(n, carry, target=target, out=out):
            block_copy(pieces[0], 0, out.at[pl.ds(0, BLK)], sems.at[target, n]).wait()
            return carry

        lax.fori_loop(0, jnp.minimum(asked[0, COUNT], ROOM), wait, 0)


def pack(here, lists, pieces):
    shape = jax.ShapeDtypeStruct((ROOM * BLK, BLK), jnp.bfloat16)
    return pl.pallas_call(
        pack_kernel,
        out_shape=(shape,) * 3,
        in_specs=[SMEM] * 4 + [ANY] * 4,
        out_specs=(VMEM,) * 3,
        scratch_shapes=[pltpu.SemaphoreType.DMA((3, ROOM))],
    )(here, *lists, *pieces)


def blank(rows):
    shape = jax.ShapeDtypeStruct((rows, BLK), jnp.bfloat16)
    return tuple(pl.pallas_call(lambda *refs: None, out_shape=(shape,) * 3, out_specs=(ANY,) * 3)())


def second_pieces(most, here, lists, pieces):
    steps = (1, -1, 2)

    def packed(pieces):
        sent = pack(here, lists, pieces)
        return tuple(second_ring(part, step) for part, step in zip(sent, steps)) + blank(4 * OUTS * BLK)

    def dense(pieces):
        near = jnp.concatenate(pieces, axis=0)
        return blank(ROOM * BLK) + tuple(second_ring(near, step) for step in steps)

    return pieces + lax.cond(most[0] <= ROOM, packed, dense, pieces)


def marks_of(array):
    return array.reshape(-1, PAY, BLK)[:, LEFT * BLK, :].astype(jnp.int32)


def local(block_values, block_columns, pattern_columns):
    row, depth, z = lax.axis_index("row"), lax.axis_index("depth"), lax.axis_index("col")
    here = jnp.stack([row % 2, row // 2 * 2 + depth % 2, depth // 2, z]).astype(jnp.int32)
    own_pattern = lax.dynamic_slice_in_dim(pattern_columns, depth * ROWS, ROWS, 0)

    marks = jnp.concatenate([block_columns.reshape(1, -1), own_pattern.reshape(1, -1)], axis=1)
    marks = jnp.pad(marks.astype(jnp.bfloat16), ((0, 15), (0, BLK - marks.shape[1])))
    values = block_values.reshape(LEFT * BLK, BLK)
    left = lax.all_gather(values, "col", axis=0, tiled=True)
    piece = lax.optimization_barrier(jnp.concatenate([values, marks], axis=0))

    near = jnp.concatenate(first_pieces(piece), axis=0)
    near, marks = lax.optimization_barrier((near, marks[:1].astype(jnp.int32)))
    near_marks = marks_of(near)
    plus, minus, far_marks = second_ring(near, 1), second_ring(near, -1), second_ring(near_marks, 2)
    row_marks = lax.all_gather(marks, "col", axis=0, tiled=True)
    plus, minus, far_marks, row_marks = lax.optimization_barrier((plus, minus, far_marks, row_marks))
    half = plus.shape[0] // 2
    plane_marks = jnp.concatenate([near_marks, marks_of(plus), marks_of(minus), far_marks], axis=0)
    ahead, behind, plane_marks = lax.optimization_barrier((plus[:half], minus[half:], plane_marks))
    far = second_ring(ahead, 1), second_ring(behind, -1)
    beside = jnp.pad(swap(plane_marks)[:, : BLK // 2], ((0, 0), (BLK // 2, 0)))
    x_jobs, s_jobs, takes = plan(here, row_marks, swap(row_marks), plane_marks + beside)
    far, x_jobs = lax.optimization_barrier((far, x_jobs))
    right = (near, plus, minus) + far
    other_right = tuple(swap(part) for part in right)
    left, x_jobs = lax.optimization_barrier((left, x_jobs))

    zero = jnp.zeros((1,), jnp.int32)
    (square,) = product(zero, x_jobs, (left,), right + other_right)
    square, left = lax.optimization_barrier((square, left))
    first, *rest = first_pieces(square)
    left_other = swap(left)
    asked = tuple(second_ring(takes[index : index + 1], step) for index, step in ((1, -1), (2, 1), (3, 2)))
    most = functools.reduce(jnp.maximum, asked, takes[:1])[0, MOST:][:1]

    stored = jnp.where((block_columns >= 0)[:, :, None, None], block_values, 0).astype(jnp.float32)
    scaled = 1.5 * jnp.pad(stored, ((0, 0), (0, KC - KA), (0, 0), (0, 0))).reshape(OUTS * BLK, BLK)
    first, scaled = lax.optimization_barrier((first, scaled))

    s_right = second_pieces(most, here, asked, (first, *rest))
    mine, theirs = product(most, s_jobs, (left, left_other), s_right)
    cube = mine.astype(jnp.float32) + swap(theirs).astype(jnp.float32)
    return (scaled - 0.5 * cube).astype(jnp.bfloat16).reshape(ROWS, KC, BLK, BLK)


def solution(mesh):
    placed = (P(("row", "depth"), "col", None, None), P(("row", "depth"), "col"), P("row", "col"))
    return jax.shard_map(
        local,
        mesh=mesh,
        in_specs=placed,
        out_specs=P(("row", "depth"), "col", None, None),
        check_vma=False,
    )
```

```python
import functools

import jax
import jax.numpy as jnp
from jax import lax
from jax.experimental import pallas as pl
from jax.experimental.pallas import tpu as pltpu
from jax.sharding import PartitionSpec as P

BLK = 128
KA = 2
KC = 3
TP = 24
ROWS = 6
OUTS = ROWS * KC
LEFT = ROWS * KA
ROOM = 22
COUNT, MOST = 32, 33
PAY = LEFT * BLK + 16
UNIT = 16
SLOTS = 32
JOBS = 2 * ROWS * 8 * KC
ALL = ("row", "col", "depth")


def chip_of(device):
    row, col, depth = device // 64, device // 8 % 8, device % 8
    return row // 2 * 2 + depth % 2, depth // 2, col, row % 2


def device_of(x, y, z, core):
    return (x // 2 * 2 + core) * 64 + z * 8 + y * 2 + x % 2


def move(array, rule):
    pairs = []
    for device in range(256):
        x, y, z, core = rule(*chip_of(device))
        pairs.append((device, device_of(x % 4, y % 4, z % 8, core)))
    return lax.ppermute(array, ALL, pairs)


def first_ring(array, step):
    return move(array, lambda x, y, z, core: (x + step * (1 - core), y + step * core, z, core))


def second_ring(array, step):
    return move(array, lambda x, y, z, core: (x + step * core, y + step * (1 - core), z, core))


def swap(array):
    return move(array, lambda x, y, z, core: (x, y, z, 1 - core))


def ring_order(away):
    away = away & 3
    return jnp.where(away == 2, 3, jnp.where(away == 3, 2, away))


def first_pieces(piece):
    far, plus, minus = [first_ring(piece, step) for step in (2, 1, -1)]
    return piece, plus, minus, far


def block_copy(ref, unit, target, sem):
    offset = pl.multiple_of(unit * UNIT, UNIT)
    return pltpu.make_async_copy(ref.at[pl.ds(offset, BLK)], target, sem)


def plan_groups(here_ref, which, group_code):
    core, x, y = here_ref[0] ^ which, here_ref[1], here_ref[2]
    first, second = jnp.where(core == 0, x, y), jnp.where(core == 0, y, x)
    for group in range(16):
        at_x, at_y = group // 8 * 2 + group % 2, group // 4 % 2 * 2 + group // 2 % 2
        far = jnp.where(core == 0, at_x, at_y)
        inner = ring_order(first - far)
        outer = ring_order(second - jnp.where(core == 0, at_y, at_x))
        group_code[0, which * 16 + group] = inner
        group_code[1, which * 16 + group] = outer
        group_code[2, which * 16 + group] = far
        group_code[3, which * 16 + group] = outer * 4 + inner


def plan_scan(marks_ref, z, panels, plane_ref, group_code, slots, add):
    def look(row, panel, base, side, wanted):
        column = marks_ref[panel, row * KA + side]
        known = jnp.maximum(column, 0)
        quarter = (known * 43) >> 8
        place = known - quarter * ROWS
        group = base + quarter
        table = group_code[3, group]
        founds = []
        for slot in range(slots):
            start = place * KA + (group & 16) * 4 if slots == KA else LEFT + place * KC
            have = plane_ref[table, start + slot]
            found = jnp.where(have == wanted[0], 0, jnp.where(have == wanted[1], 1, 2))
            founds.append(jnp.where((found < 2) | (have == wanted[2]), found, -1))
        best = jnp.where(column >= 0, functools.reduce(jnp.maximum, founds), -1)
        return best, founds, group, place

    def scan_row(row, carry):
        wanted = [marks_ref[z, LEFT + row * KC + u] for u in range(KC)]
        entries = [(panel, base, side) for panel, base in panels for side in range(KA)]
        for first in range(0, len(entries), 4):
            some = entries[first : first + 4]
            for (panel, _, side), (best, founds, group, place) in zip(some, [look(row, *entry, wanted) for entry in some]):

                @pl.when(best >= 0)
                def _(panel=panel, side=side, founds=founds, group=group, place=place):
                    left = (panel * LEFT + row * KA + side) * (BLK // UNIT)
                    inner, outer = group_code[0, group], group_code[1, group]
                    for slot, found in enumerate(founds):
                        out = row * KC + found
                        pl.when(found >= 0)(functools.partial(add, group, inner, outer, place, slot, left, out))

        return carry

    lax.fori_loop(0, ROWS, scan_row, 0)


def plan_kernel(here_ref, own_ref, other_ref, plane_ref, x_jobs, s_jobs, takes, seen, group_code):
    core, z = here_ref[0], here_ref[3]
    plan_groups(here_ref, 0, group_code)
    plan_groups(here_ref, 1, group_code)
    x_jobs[0] = 0
    s_jobs[0] = 0
    for outer in range(4):
        takes[outer, COUNT] = 0

    def clear(n, carry):
        seen[n] = -1
        return carry

    lax.fori_loop(0, 16 * OUTS, clear, 0, unroll=16)

    def add_x(group, inner, outer, place, slot, left, out):
        count = x_jobs[0]
        x_jobs[0] = count + 1
        x_jobs[1 + count] = (left << 6) | out
        source = jnp.where(outer < 3, outer, 3 + (inner >> 1)) + jnp.where(group >= 16, 5, 0)
        ahead = jnp.where(outer < 3, inner, inner & 1) * (PAY // UNIT)
        x_jobs[1 + JOBS + count] = (source << 10) | (ahead + (place * KA + slot) * (BLK // UNIT))

    def add_s(half, group, inner, outer, place, slot, left, out):
        block = place * KC + slot
        mark = group * OUTS + block

        @pl.when((outer > 0) & (seen[mark] < 0))
        def _():
            rank = takes[outer, COUNT]
            takes[outer, COUNT] = rank + 1
            seen[mark] = rank

            @pl.when(rank < ROOM)
            def _():
                takes[outer, rank] = (group_code[2, group] << 5) | block

        count = s_jobs[0]
        s_jobs[0] = count + 1
        s_jobs[1 + count] = ((half * 8 * LEFT * (BLK // UNIT) + left) << 6) | (half * OUTS + out)
        near = (inner << 10) | (block * (BLK // UNIT))
        packed = ((3 + outer) << 10) | ((seen[mark] & 31) * (BLK // UNIT))
        dense = ((6 + outer) << 10) | ((inner * OUTS + block) * (BLK // UNIT))
        s_jobs[1 + JOBS + count] = jnp.where(outer == 0, near, packed)
        s_jobs[1 + 2 * JOBS + count] = jnp.where(outer == 0, near, dense)

    def add_both(group, inner, outer, place, slot, left, out):
        add_s(0, group, inner, outer, place, slot, left, out)
        if slot < KA:
            held = plane_ref[group_code[3, group], place * KA + slot] >= 0
            pl.when(held)(functools.partial(add_x, group, inner, outer, place, slot, left, out))

    panels = [(panel // 2 * 4 + 2 * core + panel % 2, panel * 4) for panel in range(4)]
    plan_scan(own_ref, z, panels, plane_ref, group_code, KC, add_both)
    plan_scan(other_ref, z, panels, plane_ref, group_code, KC, functools.partial(add_s, 1))
    panels = [(panel // 2 * 4 + 2 * (1 - core) + panel % 2, 16 + panel * 4) for panel in range(4)]
    plan_scan(own_ref, z, panels, plane_ref, group_code, KA, add_x)
    most = jnp.maximum(takes[1, COUNT], jnp.maximum(takes[2, COUNT], takes[3, COUNT]))
    for outer in range(4):
        takes[outer, MOST] = most


SMEM = pl.BlockSpec(memory_space=pltpu.SMEM)
VMEM = pl.BlockSpec(memory_space=pltpu.VMEM)
ANY = pl.BlockSpec(memory_space=pl.ANY)


SMALL = pl.CostEstimate(flops=1000, bytes_accessed=1000, transcendentals=0)
JOB_TABLE = jax.ShapeDtypeStruct((1 + 3 * JOBS,), jnp.int32)


def plan(here, own, other, plane):
    return pl.pallas_call(
        plan_kernel,
        out_shape=(JOB_TABLE, JOB_TABLE, jax.ShapeDtypeStruct((4, BLK), jnp.int32)),
        in_specs=[SMEM] * 4,
        out_specs=(SMEM,) * 3,
        scratch_shapes=[pltpu.SMEM((16 * OUTS,), jnp.int32), pltpu.SMEM((4, 32), jnp.int32)],
        cost_estimate=SMALL,
    )(here, own, other, plane)


def product_kernel(lefts, rights, most_ref, jobs_ref, *refs):
    left_refs, right_refs, refs = refs[:lefts], refs[lefts : lefts + rights], refs[lefts + rights :]
    outs_refs, (total, left_buf, right_buf, sems) = refs[:lefts], refs[lefts:]
    count = jobs_ref[0]
    codes = jnp.where(most_ref[0] <= ROOM, 1 + JOBS, 1 + 2 * JOBS)

    def start(n):
        slot = n & (SLOTS - 1)
        left = jobs_ref[1 + n] >> 6
        code = jobs_ref[codes + n]
        source, unit = code >> 10, code & 1023
        whole = 8 * LEFT * (BLK // UNIT)
        for index, ref in enumerate(left_refs):

            @pl.when((left >= index * whole) & (left < (index + 1) * whole))
            def _(ref=ref, index=index):
                block_copy(ref, left - index * whole, left_buf.at[slot], sems.at[0, slot]).start()

        def right(low, high):
            if high - low == 1:
                block_copy(right_refs[low], unit, right_buf.at[slot], sems.at[1, slot]).start()
            else:
                middle = (low + high) // 2
                pl.when(source < middle)(functools.partial(right, low, middle))
                pl.when(source >= middle)(functools.partial(right, middle, high))

        right(0, rights)

    def wait(n):
        slot = n & (SLOTS - 1)
        block_copy(left_refs[0], 0, left_buf.at[slot], sems.at[0, slot]).wait()
        block_copy(left_refs[0], 0, right_buf.at[slot], sems.at[1, slot]).wait()

    def first(n, carry):
        start(n)
        return carry

    lax.fori_loop(0, jnp.minimum(count, SLOTS), first, 0)
    total[...] = jnp.zeros_like(total)

    def multiply(group, carry):
        at = [group * 4 + index for index in range(4)]
        for n in at:
            pl.when(n < count)(functools.partial(wait, n))
        outs = [jnp.where(n < count, jobs_ref[jnp.minimum(1 + n, JOBS)] & 63, lefts * OUTS) for n in at]
        slots = [n & (SLOTS - 1) for n in at]
        dots = [jnp.dot(left_buf[slot], right_buf[slot], preferred_element_type=jnp.float32) for slot in slots]
        for out, dot in zip(outs, dots):
            total[out] += dot
        for n in at:
            pl.when(n + SLOTS < count)(functools.partial(start, n + SLOTS))
        return carry

    lax.fori_loop(0, (count + 3) // 4, multiply, 0)
    for half, ref in enumerate(outs_refs):
        for block in range(OUTS):
            ref[pl.ds(block * BLK, BLK), :] = total[half * OUTS + block].astype(jnp.bfloat16)


def product(most, jobs, lefts, rights):
    return pl.pallas_call(
        functools.partial(product_kernel, len(lefts), len(rights)),
        out_shape=(jax.ShapeDtypeStruct((OUTS * BLK, BLK), jnp.bfloat16),) * len(lefts),
        in_specs=[SMEM] * 2 + [ANY] * (len(lefts) + len(rights)),
        out_specs=(VMEM,) * len(lefts),
        scratch_shapes=[
            pltpu.VMEM((len(lefts) * OUTS + 1, BLK, BLK), jnp.float32),
            pltpu.VMEM((SLOTS, BLK, BLK), jnp.bfloat16),
            pltpu.VMEM((SLOTS, BLK, BLK), jnp.bfloat16),
            pltpu.SemaphoreType.DMA((2, SLOTS)),
        ],
        compiler_params=pltpu.CompilerParams(vmem_limit_bytes=7 * 1024 * 1024),
    )(most, jobs, *lefts, *rights)


def pack_kernel(here_ref, *refs):
    lists, pieces, outs, sems = refs[:3], refs[3:7], refs[7:10], refs[10]
    first = jnp.where(here_ref[0] == 0, here_ref[1], here_ref[2])

    for target, (asked, out) in enumerate(zip(lists, outs)):

        def start(n, carry, target=target, out=out, asked=asked):
            code = asked[0, n]
            inner = ring_order(first - (code >> 5))
            offset = pl.multiple_of(n * BLK, BLK)
            for index, ref in enumerate(pieces):

                @pl.when(inner == index)
                def _(ref=ref):
                    block_copy(ref, (code & 31) * (BLK // UNIT), out.at[pl.ds(offset, BLK)], sems.at[target, n]).start()

            return carry

        lax.fori_loop(0, jnp.minimum(asked[0, COUNT], ROOM), start, 0)

    for target, (asked, out) in enumerate(zip(lists, outs)):

        def wait(n, carry, target=target, out=out):
            block_copy(pieces[0], 0, out.at[pl.ds(0, BLK)], sems.at[target, n]).wait()
            return carry

        lax.fori_loop(0, jnp.minimum(asked[0, COUNT], ROOM), wait, 0)


def pack(here, lists, pieces):
    shape = jax.ShapeDtypeStruct((ROOM * BLK, BLK), jnp.bfloat16)
    return pl.pallas_call(
        pack_kernel,
        out_shape=(shape,) * 3,
        in_specs=[SMEM] * 4 + [ANY] * 4,
        out_specs=(VMEM,) * 3,
        scratch_shapes=[pltpu.SemaphoreType.DMA((3, ROOM))],
    )(here, *lists, *pieces)


def blank(rows):
    shape = jax.ShapeDtypeStruct((rows, BLK), jnp.bfloat16)
    return tuple(pl.pallas_call(lambda *refs: None, out_shape=(shape,) * 3, out_specs=(ANY,) * 3)())


def second_pieces(most, here, lists, pieces):
    steps = (1, -1, 2)

    def packed(pieces):
        sent = pack(here, lists, pieces)
        return tuple(second_ring(part, step) for part, step in zip(sent, steps)) + blank(4 * OUTS * BLK)

    def dense(pieces):
        near = jnp.concatenate(pieces, axis=0)
        return blank(ROOM * BLK) + tuple(second_ring(near, step) for step in steps)

    return pieces + lax.cond(most[0] <= ROOM, packed, dense, pieces)


def marks_of(array):
    return array.reshape(-1, PAY, BLK)[:, LEFT * BLK, :].astype(jnp.int32)


def local(block_values, block_columns, pattern_columns):
    row, depth, z = lax.axis_index("row"), lax.axis_index("depth"), lax.axis_index("col")
    here = jnp.stack([row % 2, row // 2 * 2 + depth % 2, depth // 2, z]).astype(jnp.int32)
    own_pattern = lax.dynamic_slice_in_dim(pattern_columns, depth * ROWS, ROWS, 0)

    marks = jnp.concatenate([block_columns.reshape(1, -1), own_pattern.reshape(1, -1)], axis=1)
    marks = jnp.pad(marks.astype(jnp.bfloat16), ((0, 15), (0, BLK - marks.shape[1])))
    values = block_values.reshape(LEFT * BLK, BLK)
    left = lax.all_gather(values, "col", axis=0, tiled=True)
    piece = lax.optimization_barrier(jnp.concatenate([values, marks], axis=0))

    near = jnp.concatenate(first_pieces(piece), axis=0)
    near, marks = lax.optimization_barrier((near, marks[:1].astype(jnp.int32)))
    near_marks = marks_of(near)
    plus, minus, far_marks = second_ring(near, 1), second_ring(near, -1), second_ring(near_marks, 2)
    row_marks = lax.all_gather(marks, "col", axis=0, tiled=True)
    plus, minus, far_marks, row_marks = lax.optimization_barrier((plus, minus, far_marks, row_marks))
    half = plus.shape[0] // 2
    plane_marks = jnp.concatenate([near_marks, marks_of(plus), marks_of(minus), far_marks], axis=0)
    ahead, behind, plane_marks = lax.optimization_barrier((plus[:half], minus[half:], plane_marks))
    far = second_ring(ahead, 1), second_ring(behind, -1)
    beside = jnp.pad(swap(plane_marks)[:, : BLK // 2], ((0, 0), (BLK // 2, 0)))
    x_jobs, s_jobs, takes = plan(here, row_marks, swap(row_marks), plane_marks + beside)
    far, x_jobs = lax.optimization_barrier((far, x_jobs))
    right = (near, plus, minus) + far
    other_right = tuple(swap(part) for part in right)
    left, x_jobs = lax.optimization_barrier((left, x_jobs))

    zero = jnp.zeros((1,), jnp.int32)
    (square,) = product(zero, x_jobs, (left,), right + other_right)
    square, left = lax.optimization_barrier((square, left))
    first, *rest = first_pieces(square)
    left_other = swap(left)
    asked = tuple(second_ring(takes[index : index + 1], step) for index, step in ((1, -1), (2, 1), (3, 2)))
    most = functools.reduce(jnp.maximum, asked, takes[:1])[0, MOST:][:1]

    stored = jnp.where((block_columns >= 0)[:, :, None, None], block_values, 0).astype(jnp.float32)
    scaled = 1.5 * jnp.pad(stored, ((0, 0), (0, KC - KA), (0, 0), (0, 0))).reshape(OUTS * BLK, BLK)
    first, scaled = lax.optimization_barrier((first, scaled))

    s_right = second_pieces(most, here, asked, (first, *rest))
    mine, theirs = product(most, s_jobs, (left, left_other), s_right)
    cube = mine.astype(jnp.float32) + swap(theirs).astype(jnp.float32)
    return (scaled - 0.5 * cube).astype(jnp.bfloat16).reshape(ROWS, KC, BLK, BLK)


def solution(mesh):
    placed = (P(("row", "depth"), "col", None, None), P(("row", "depth"), "col"), P("row", "col"))
    return jax.shard_map(
        local,
        mesh=mesh,
        in_specs=placed,
        out_specs=P(("row", "depth"), "col", None, None),
        check_vma=False,
    )
```

```python
import functools

import jax
import jax.numpy as jnp
from jax import lax
from jax.experimental import pallas as pl
from jax.experimental.pallas import tpu as pltpu
from jax.sharding import PartitionSpec as P

BLK = 128
KA = 2
KC = 3
TP = 24
ROWS = 6
OUTS = ROWS * KC
LEFT = ROWS * KA
ROOM = 22
COUNT, MOST = 32, 33
PAY = LEFT * BLK + 16
UNIT = 16
SLOTS = 16
JOBS = 2 * ROWS * 8 * KC
ALL = ("row", "col", "depth")


def chip_of(device):
    row, col, depth = device // 64, device // 8 % 8, device % 8
    return row // 2 * 2 + depth % 2, depth // 2, col, row % 2


def device_of(x, y, z, core):
    return (x // 2 * 2 + core) * 64 + z * 8 + y * 2 + x % 2


def move(array, rule):
    pairs = []
    for device in range(256):
        x, y, z, core = rule(*chip_of(device))
        pairs.append((device, device_of(x % 4, y % 4, z % 8, core)))
    return lax.ppermute(array, ALL, pairs)


def first_ring(array, step):
    return move(array, lambda x, y, z, core: (x + step * (1 - core), y + step * core, z, core))


def second_ring(array, step):
    return move(array, lambda x, y, z, core: (x + step * core, y + step * (1 - core), z, core))


def swap(array):
    return move(array, lambda x, y, z, core: (x, y, z, 1 - core))


def ring_order(away):
    away = away & 3
    return jnp.where(away == 2, 3, jnp.where(away == 3, 2, away))


def first_pieces(piece):
    far, plus, minus = [first_ring(piece, step) for step in (2, 1, -1)]
    return piece, plus, minus, far


def block_copy(ref, unit, target, sem):
    offset = pl.multiple_of(unit * UNIT, UNIT)
    return pltpu.make_async_copy(ref.at[pl.ds(offset, BLK)], target, sem)


def plan_groups(here_ref, which, group_code):
    core, x, y = here_ref[0] ^ which, here_ref[1], here_ref[2]
    first, second = jnp.where(core == 0, x, y), jnp.where(core == 0, y, x)
    for group in range(16):
        at_x, at_y = group // 8 * 2 + group % 2, group // 4 % 2 * 2 + group // 2 % 2
        far = jnp.where(core == 0, at_x, at_y)
        inner = ring_order(first - far)
        outer = ring_order(second - jnp.where(core == 0, at_y, at_x))
        group_code[0, which * 16 + group] = inner
        group_code[1, which * 16 + group] = outer
        group_code[2, which * 16 + group] = far
        group_code[3, which * 16 + group] = outer * 4 + inner


def plan_scan(marks_ref, z, panels, plane_ref, group_code, slots, add):
    def look(row, panel, base, side, wanted):
        column = marks_ref[panel, row * KA + side]
        known = jnp.maximum(column, 0)
        quarter = (known * 43) >> 8
        place = known - quarter * ROWS
        group = base + quarter
        table = group_code[3, group]
        founds = []
        for slot in range(slots):
            start = place * KA + (group & 16) * 4 if slots == KA else LEFT + place * KC
            have = plane_ref[table, start + slot]
            found = jnp.where(have == wanted[0], 0, jnp.where(have == wanted[1], 1, 2))
            founds.append(jnp.where((found < 2) | (have == wanted[2]), found, -1))
        best = jnp.where(column >= 0, functools.reduce(jnp.maximum, founds), -1)
        return best, founds, group, place

    def scan_row(row, carry):
        wanted = [marks_ref[z, LEFT + row * KC + u] for u in range(KC)]
        entries = [(panel, base, side) for panel, base in panels for side in range(KA)]
        for first in range(0, len(entries), 4):
            some = entries[first : first + 4]
            for (panel, _, side), (best, founds, group, place) in zip(some, [look(row, *entry, wanted) for entry in some]):

                @pl.when(best >= 0)
                def _(panel=panel, side=side, founds=founds, group=group, place=place):
                    left = (panel * LEFT + row * KA + side) * (BLK // UNIT)
                    inner, outer = group_code[0, group], group_code[1, group]
                    for slot, found in enumerate(founds):
                        out = row * KC + found
                        pl.when(found >= 0)(functools.partial(add, group, inner, outer, place, slot, left, out))

        return carry

    lax.fori_loop(0, ROWS, scan_row, 0)


def plan_kernel(here_ref, own_ref, other_ref, plane_ref, x_jobs, s_jobs, takes, seen, group_code):
    core, z = here_ref[0], here_ref[3]
    plan_groups(here_ref, 0, group_code)
    plan_groups(here_ref, 1, group_code)
    x_jobs[0] = 0
    s_jobs[0] = 0
    for outer in range(4):
        takes[outer, COUNT] = 0

    def clear(n, carry):
        seen[n] = -1
        return carry

    lax.fori_loop(0, 16 * OUTS, clear, 0, unroll=16)

    def add_x(group, inner, outer, place, slot, left, out):
        count = x_jobs[0]
        x_jobs[0] = count + 1
        x_jobs[1 + count] = (left << 6) | out
        source = jnp.where(outer < 3, outer, 3 + (inner >> 1)) + jnp.where(group >= 16, 5, 0)
        ahead = jnp.where(outer < 3, inner, inner & 1) * (PAY // UNIT)
        x_jobs[1 + JOBS + count] = (source << 10) | (ahead + (place * KA + slot) * (BLK // UNIT))

    def add_s(half, group, inner, outer, place, slot, left, out):
        block = place * KC + slot
        mark = group * OUTS + block

        @pl.when((outer > 0) & (seen[mark] < 0))
        def _():
            rank = takes[outer, COUNT]
            takes[outer, COUNT] = rank + 1
            seen[mark] = rank

            @pl.when(rank < ROOM)
            def _():
                takes[outer, rank] = (group_code[2, group] << 5) | block

        count = s_jobs[0]
        s_jobs[0] = count + 1
        s_jobs[1 + count] = ((half * 8 * LEFT * (BLK // UNIT) + left) << 6) | (half * OUTS + out)
        near = (inner << 10) | (block * (BLK // UNIT))
        packed = ((3 + outer) << 10) | ((seen[mark] & 31) * (BLK // UNIT))
        dense = ((6 + outer) << 10) | ((inner * OUTS + block) * (BLK // UNIT))
        s_jobs[1 + JOBS + count] = jnp.where(outer == 0, near, packed)
        s_jobs[1 + 2 * JOBS + count] = jnp.where(outer == 0, near, dense)

    def add_both(group, inner, outer, place, slot, left, out):
        add_s(0, group, inner, outer, place, slot, left, out)
        if slot < KA:
            held = plane_ref[group_code[3, group], place * KA + slot] >= 0
            pl.when(held)(functools.partial(add_x, group, inner, outer, place, slot, left, out))

    panels = [(panel // 2 * 4 + 2 * core + panel % 2, panel * 4) for panel in range(4)]
    plan_scan(own_ref, z, panels, plane_ref, group_code, KC, add_both)
    plan_scan(other_ref, z, panels, plane_ref, group_code, KC, functools.partial(add_s, 1))
    panels = [(panel // 2 * 4 + 2 * (1 - core) + panel % 2, 16 + panel * 4) for panel in range(4)]
    plan_scan(own_ref, z, panels, plane_ref, group_code, KA, add_x)
    most = jnp.maximum(takes[1, COUNT], jnp.maximum(takes[2, COUNT], takes[3, COUNT]))
    for outer in range(4):
        takes[outer, MOST] = most


SMEM = pl.BlockSpec(memory_space=pltpu.SMEM)
VMEM = pl.BlockSpec(memory_space=pltpu.VMEM)
ANY = pl.BlockSpec(memory_space=pl.ANY)


SMALL = pl.CostEstimate(flops=1000, bytes_accessed=1000, transcendentals=0)
JOB_TABLE = jax.ShapeDtypeStruct((1 + 3 * JOBS,), jnp.int32)


def plan(here, own, other, plane):
    return pl.pallas_call(
        plan_kernel,
        out_shape=(JOB_TABLE, JOB_TABLE, jax.ShapeDtypeStruct((4, BLK), jnp.int32)),
        in_specs=[SMEM] * 4,
        out_specs=(SMEM,) * 3,
        scratch_shapes=[pltpu.SMEM((16 * OUTS,), jnp.int32), pltpu.SMEM((4, 32), jnp.int32)],
        cost_estimate=SMALL,
    )(here, own, other, plane)


def product_kernel(lefts, rights, most_ref, jobs_ref, *refs):
    left_refs, right_refs, refs = refs[:lefts], refs[lefts : lefts + rights], refs[lefts + rights :]
    outs_refs, (total, left_buf, right_buf, sems) = refs[:lefts], refs[lefts:]
    count = jobs_ref[0]
    codes = jnp.where(most_ref[0] <= ROOM, 1 + JOBS, 1 + 2 * JOBS)

    def start(n):
        slot = n & (SLOTS - 1)
        left = jobs_ref[1 + n] >> 6
        code = jobs_ref[codes + n]
        source, unit = code >> 10, code & 1023
        whole = 8 * LEFT * (BLK // UNIT)
        for index, ref in enumerate(left_refs):

            @pl.when((left >= index * whole) & (left < (index + 1) * whole))
            def _(ref=ref, index=index):
                block_copy(ref, left - index * whole, left_buf.at[slot], sems.at[0, slot]).start()

        def right(low, high):
            if high - low == 1:
                block_copy(right_refs[low], unit, right_buf.at[slot], sems.at[1, slot]).start()
            else:
                middle = (low + high) // 2
                pl.when(source < middle)(functools.partial(right, low, middle))
                pl.when(source >= middle)(functools.partial(right, middle, high))

        right(0, rights)

    def wait(n):
        slot = n & (SLOTS - 1)
        block_copy(left_refs[0], 0, left_buf.at[slot], sems.at[0, slot]).wait()
        block_copy(left_refs[0], 0, right_buf.at[slot], sems.at[1, slot]).wait()

    def first(n, carry):
        start(n)
        return carry

    lax.fori_loop(0, jnp.minimum(count, SLOTS), first, 0)
    total[...] = jnp.zeros_like(total)

    def multiply(group, carry):
        at = [group * 4 + index for index in range(4)]
        for n in at:
            pl.when(n < count)(functools.partial(wait, n))
        outs = [jnp.where(n < count, jobs_ref[jnp.minimum(1 + n, JOBS)] & 63, lefts * OUTS) for n in at]
        slots = [n & (SLOTS - 1) for n in at]
        dots = [jnp.dot(left_buf[slot], right_buf[slot], preferred_element_type=jnp.float32) for slot in slots]
        for out, dot in zip(outs, dots):
            total[out] += dot
        for n in at:
            pl.when(n + SLOTS < count)(functools.partial(start, n + SLOTS))
        return carry

    lax.fori_loop(0, (count + 3) // 4, multiply, 0)
    for half, ref in enumerate(outs_refs):
        for block in range(OUTS):
            ref[pl.ds(block * BLK, BLK), :] = total[half * OUTS + block].astype(jnp.bfloat16)


def product(most, jobs, lefts, rights):
    return pl.pallas_call(
        functools.partial(product_kernel, len(lefts), len(rights)),
        out_shape=(jax.ShapeDtypeStruct((OUTS * BLK, BLK), jnp.bfloat16),) * len(lefts),
        in_specs=[SMEM] * 2 + [ANY] * (len(lefts) + len(rights)),
        out_specs=(VMEM,) * len(lefts),
        scratch_shapes=[
            pltpu.VMEM((len(lefts) * OUTS + 1, BLK, BLK), jnp.float32),
            pltpu.VMEM((SLOTS, BLK, BLK), jnp.bfloat16),
            pltpu.VMEM((SLOTS, BLK, BLK), jnp.bfloat16),
            pltpu.SemaphoreType.DMA((2, SLOTS)),
        ],
        compiler_params=pltpu.CompilerParams(vmem_limit_bytes=6 * 1024 * 1024),
    )(most, jobs, *lefts, *rights)


def pack_kernel(here_ref, *refs):
    lists, pieces, outs, sems = refs[:3], refs[3:7], refs[7:10], refs[10]
    first = jnp.where(here_ref[0] == 0, here_ref[1], here_ref[2])

    for target, (asked, out) in enumerate(zip(lists, outs)):

        def start(n, carry, target=target, out=out, asked=asked):
            code = asked[0, n]
            inner = ring_order(first - (code >> 5))
            offset = pl.multiple_of(n * BLK, BLK)
            for index, ref in enumerate(pieces):

                @pl.when(inner == index)
                def _(ref=ref):
                    block_copy(ref, (code & 31) * (BLK // UNIT), out.at[pl.ds(offset, BLK)], sems.at[target, n]).start()

            return carry

        lax.fori_loop(0, jnp.minimum(asked[0, COUNT], ROOM), start, 0)

    for target, (asked, out) in enumerate(zip(lists, outs)):

        def wait(n, carry, target=target, out=out):
            block_copy(pieces[0], 0, out.at[pl.ds(0, BLK)], sems.at[target, n]).wait()
            return carry

        lax.fori_loop(0, jnp.minimum(asked[0, COUNT], ROOM), wait, 0)


def pack(here, lists, pieces):
    shape = jax.ShapeDtypeStruct((ROOM * BLK, BLK), jnp.bfloat16)
    return pl.pallas_call(
        pack_kernel,
        out_shape=(shape,) * 3,
        in_specs=[SMEM] * 4 + [ANY] * 4,
        out_specs=(VMEM,) * 3,
        scratch_shapes=[pltpu.SemaphoreType.DMA((3, ROOM))],
    )(here, *lists, *pieces)


def blank(rows):
    shape = jax.ShapeDtypeStruct((rows, BLK), jnp.bfloat16)
    return tuple(pl.pallas_call(lambda *refs: None, out_shape=(shape,) * 3, out_specs=(ANY,) * 3)())


def second_pieces(most, here, lists, pieces):
    steps = (1, -1, 2)

    def packed(pieces):
        sent = pack(here, lists, pieces)
        return tuple(second_ring(part, step) for part, step in zip(sent, steps)) + blank(4 * OUTS * BLK)

    def dense(pieces):
        near = jnp.concatenate(pieces, axis=0)
        return blank(ROOM * BLK) + tuple(second_ring(near, step) for step in steps)

    return pieces + lax.cond(most[0] <= ROOM, packed, dense, pieces)


def marks_of(array):
    return array.reshape(-1, PAY, BLK)[:, LEFT * BLK, :].astype(jnp.int32)


def local(block_values, block_columns, pattern_columns):
    row, depth, z = lax.axis_index("row"), lax.axis_index("depth"), lax.axis_index("col")
    here = jnp.stack([row % 2, row // 2 * 2 + depth % 2, depth // 2, z]).astype(jnp.int32)
    own_pattern = lax.dynamic_slice_in_dim(pattern_columns, depth * ROWS, ROWS, 0)

    marks = jnp.concatenate([block_columns.reshape(1, -1), own_pattern.reshape(1, -1)], axis=1)
    marks = jnp.pad(marks.astype(jnp.bfloat16), ((0, 15), (0, BLK - marks.shape[1])))
    values = block_values.reshape(LEFT * BLK, BLK)
    left = lax.all_gather(values, "col", axis=0, tiled=True)
    piece = lax.optimization_barrier(jnp.concatenate([values, marks], axis=0))

    near = jnp.concatenate(first_pieces(piece), axis=0)
    near, marks = lax.optimization_barrier((near, marks[:1].astype(jnp.int32)))
    near_marks = marks_of(near)
    plus, minus, far_marks = second_ring(near, 1), second_ring(near, -1), second_ring(near_marks, 2)
    row_marks = lax.all_gather(marks, "col", axis=0, tiled=True)
    plus, minus, far_marks, row_marks = lax.optimization_barrier((plus, minus, far_marks, row_marks))
    half = plus.shape[0] // 2
    plane_marks = jnp.concatenate([near_marks, marks_of(plus), marks_of(minus), far_marks], axis=0)
    ahead, behind, plane_marks = lax.optimization_barrier((plus[:half], minus[half:], plane_marks))
    far = second_ring(ahead, 1), second_ring(behind, -1)
    beside = jnp.pad(swap(plane_marks)[:, : BLK // 2], ((0, 0), (BLK // 2, 0)))
    x_jobs, s_jobs, takes = plan(here, row_marks, swap(row_marks), plane_marks + beside)
    far, x_jobs = lax.optimization_barrier((far, x_jobs))
    right = (near, plus, minus) + far
    other_right = tuple(swap(part) for part in right)
    left, x_jobs = lax.optimization_barrier((left, x_jobs))

    zero = jnp.zeros((1,), jnp.int32)
    (square,) = product(zero, x_jobs, (left,), right + other_right)
    square, left = lax.optimization_barrier((square, left))
    first, *rest = first_pieces(square)
    left_other = swap(left)
    asked = tuple(second_ring(takes[index : index + 1], step) for index, step in ((1, -1), (2, 1), (3, 2)))
    most = functools.reduce(jnp.maximum, asked, takes[:1])[0, MOST:][:1]

    stored = jnp.where((block_columns >= 0)[:, :, None, None], block_values, 0).astype(jnp.float32)
    scaled = 1.5 * jnp.pad(stored, ((0, 0), (0, KC - KA), (0, 0), (0, 0))).reshape(OUTS * BLK, BLK)
    first, scaled = lax.optimization_barrier((first, scaled))

    s_right = second_pieces(most, here, asked, (first, *rest))
    mine, theirs = product(most, s_jobs, (left, left_other), s_right)
    cube = mine.astype(jnp.float32) + swap(theirs).astype(jnp.float32)
    return (scaled - 0.5 * cube).astype(jnp.bfloat16).reshape(ROWS, KC, BLK, BLK)


def solution(mesh):
    placed = (P(("row", "depth"), "col", None, None), P(("row", "depth"), "col"), P("row", "col"))
    return jax.shard_map(
        local,
        mesh=mesh,
        in_specs=placed,
        out_specs=P(("row", "depth"), "col", None, None),
        check_vma=False,
    )
```
